512 devices in a mesh: shard: 128 (over z, x, core), split: 4 (over y).
Axes of the slice: x: 4, y: 4, z: 16, core: 2. Of those that a mesh axis runs over, the one named last changes fastest.
Arguments:
- embeddings: bfloat16 [65536, 768], P(('shard', 'split')), may hold values from -160 to 160
- labels: int32 [65536], P(('shard', 'split')), may hold values from 0 to 1023, as said below
Outputs:
- weight: float32 [65536], P(('shard', 'split'))
The draws below stay inside these ranges and needn't reach their ends.
Inputs may be any that keep to these rules, and one draw needn't show every extreme that they name: `labels`: cluster c belongs to owner c integer-divided by 8. On each device, the rows name the clusters of any one owner at most 4 times; on every device some owner is named exactly 4 times, and one owner is named 4 times on every device.
All inputs are finite; a program needn't handle non-finite values.
Results may differ from the reference program's by a relative error of at most 0.00041.
Values may be sent and summed in bfloat16 or wider, within the bound.
A program may use at most 64 MiB of HBM per device.

```python
import jax
import jax.numpy as jnp
from jax import lax

D = 768
DOC_DEV = 128
CL_OWN = 8
CAP = 4
CLUSTERS = 1024
DOCS = 65536
N_SHARD = 128
N_SPLIT = 4


def common_draw(key):
    slots = N_SHARD * CAP
    tier = jax.random.randint(jax.random.fold_in(key, 12), (N_SHARD,), 0, 3).astype(jnp.int32)
    fixed_owner = jax.random.randint(jax.random.fold_in(key, 13), (), 0, N_SHARD).astype(jnp.int32)
    slot_owner = jnp.arange(slots, dtype=jnp.int32) // CAP

    def one_block(block_key):
        first, second, third, fourth = jax.random.split(block_key, 4)
        own_owner = jax.random.randint(first, (), 0, N_SHARD).astype(jnp.int32)
        forced = ((slot_owner == fixed_owner) | (slot_owner == own_owner)).astype(jnp.int32)
        rough = jax.random.randint(second, (slots,), 0, 1024).astype(jnp.int32)
        score = (rough + tier[slot_owner] * 256 + forced * 4096) * slots + jnp.arange(slots, dtype=jnp.int32)
        _, picked = lax.top_k(score, DOC_DEV)
        owners = jax.random.permutation(third, slot_owner[picked])
        inner = jax.random.randint(fourth, (DOC_DEV,), 0, CL_OWN).astype(jnp.int32)
        return owners * CL_OWN + inner
    block_keys = jax.random.split(jax.random.fold_in(key, 14), N_SHARD * N_SPLIT)
    labels = jax.vmap(one_block)(block_keys).reshape(-1).astype(jnp.int32)
    return labels


def draw_labels(key, part):
    return common_draw(key)


def draw_embeddings(key, part):
    labels = common_draw(key)
    key = jax.random.fold_in(key, 21)
    first, second, third, fourth = jax.random.split(key, 4)
    fifth, sixth, seventh, eighth = jax.random.split(jax.random.fold_in(key, 5), 4)
    centre = jax.random.truncated_normal(first, -4.0, 4.0, (CLUSTERS, D), jnp.float32)
    strength = jax.random.uniform(second, (CLUSTERS,), jnp.float32, 0.7, 1.3)
    noise = jax.random.truncated_normal(third, -4.0, 4.0, (DOCS, D), jnp.float32)
    template_noise = jax.random.truncated_normal(fifth, -4.0, 4.0, (CLUSTERS, 4, D), jnp.float32)
    scale = jnp.exp(jax.random.uniform(fourth, (DOCS, 1), jnp.float32, 0.0, 2.3))
    base = strength[labels][:, None] * centre[labels]
    templates = strength[:, None, None] * centre[:, None, :] + template_noise
    pick = jax.random.randint(sixth, (DOCS,), 0, 4).astype(jnp.int32)
    copied = jax.random.randint(seventh, (DOCS,), 0, 10).astype(jnp.int32) < 3
    spread = jax.random.uniform(eighth, (DOCS, 1), jnp.float32, 0.1, 0.4)
    copy_rows = templates[labels, pick] + spread * noise
    rows = jnp.where(copied[:, None], copy_rows, base + noise) * scale
    return rows.astype(jnp.bfloat16)


def setup_inputs(seed: int = 0) -> dict:
    seeds = jax.random.split(jax.random.key(seed), 3)
    embeddings = draw_embeddings(jax.random.fold_in(seeds[2], 71), 0)
    labels = draw_labels(jax.random.fold_in(seeds[2], 71), 0)
    return {"embeddings": embeddings, "labels": labels}


inverse_temp = 10.0

def reference(embeddings, labels):
    docs = embeddings.shape[0]
    wide = embeddings.astype(jnp.float32)
    norm_sq = lax.optimization_barrier(jnp.sum(wide * wide, axis=1, keepdims=True)) + 1e-06
    unit = (wide * lax.rsqrt(norm_sq)).astype(jnp.bfloat16)
    owner = (labels // CL_OWN).astype(jnp.int32)
    order = jnp.argsort(owner, stable=True).astype(jnp.int32)
    owner_ids = jnp.arange(N_SHARD, dtype=jnp.int32)
    counts = lax.optimization_barrier(jnp.sum((owner[None, :] == owner_ids[:, None]).astype(jnp.int32), axis=1))
    offsets = (jnp.cumsum(counts) - counts).astype(jnp.int32)
    window = N_SHARD * N_SPLIT * CAP
    padded_unit = jnp.concatenate([unit[order], jnp.zeros((window, D), jnp.bfloat16)], axis=0)
    padded_lab = jnp.concatenate([labels[order], jnp.full((window,), -1, jnp.int32)], axis=0)

    def one_owner(carry, index):
        start = offsets[index].astype(jnp.int32)
        count = counts[index]
        rows = lax.dynamic_slice_in_dim(padded_unit, start, window, 0)
        labs = lax.dynamic_slice_in_dim(padded_lab, start, window, 0)
        live = jnp.arange(window, dtype=jnp.int32) < count
        sims = jnp.dot(rows, rows.T, preferred_element_type=jnp.float32)
        same = (labs[:, None] == labs[None, :]) & live[None, :]
        totals = lax.optimization_barrier(jnp.sum(jnp.where(same, jnp.exp(inverse_temp * sims), jnp.float32(0.0)), axis=1))
        older = lax.dynamic_slice_in_dim(carry, start, window, 0)
        carry = lax.dynamic_update_slice_in_dim(carry, jnp.where(live, totals, older), start, 0)
        return (carry, None)
    initial = jnp.ones((docs + window,), jnp.float32)
    sorted_totals, _ = lax.scan(one_owner, initial, owner_ids)
    totals = jnp.zeros((docs,), jnp.float32).at[order].set(sorted_totals[:docs])
    return 0.1 * jnp.log(totals)
```

```python
import functools

import jax
import jax.numpy as jnp
from jax import lax
from jax.experimental import pallas as pl
from jax.experimental.pallas import tpu as pltpu
from jax.sharding import PartitionSpec as P

MESH = pl.DeviceIdType.MESH
F32 = jnp.float32
BF16 = jnp.bfloat16

D = 768
EXT = 128
WIDE = D + EXT
ROWS = 128
NZ, NX, NY = 16, 4, 4
PIECE = 64
PENALTY = 16.0
LOG2E10 = 14.426950408889634


def one_hot(cond):
    return jnp.where(cond, 1.0, 0.0).astype(BF16)


def dot_nn(a, b):
    return lax.dot_general(a, b, (((1,), (0,)), ((), ())), preferred_element_type=F32)


def dot_nt(a, b):
    return lax.dot_general(a, b, (((1,), (1,)), ((), ())), preferred_element_type=F32)


def iota(shape, dim):
    return lax.broadcasted_iota(jnp.int32, shape, dim)


def kernel(
    emb_ref, lab_ref, out_ref,
    unit, raw, fsend, farr, meta, psend, own, sib, left, acc, colacc, tot, back, ret, wts,
    raw_send, raw_recv, far_send, far_recv, meta_send, meta_recv, plane_send, own_recv,
    sib_send, sib_recv, tot_send, tot_recv, ret_send, ret_recv,
):
    p = lax.axis_index("shard")
    y = lax.axis_index("split")
    z = p // 8
    x = (p % 8) // 2
    c = p % 2
    xy = x * NY + y
    turn = (y - x + NY) % NY
    handles = turn % 2 == 0
    my_owner = x * 2 + turn // 2

    def at(zz, xx, cc, yy):
        return (zz * 8 + xx * 2 + cc, yy)

    def handler_y(j):
        return (2 * (j % 2) + j // 2) % NY

    def up(pos):
        k = (pos + 1) // 2
        return (z + jnp.where(pos % 2 == 1, k, NZ - k)) % NZ

    def down(pos):
        k = (pos + 1) // 2
        return (z + jnp.where(pos % 2 == 1, NZ - k, k)) % NZ

    barrier = pltpu.get_barrier_semaphore()

    def greet(device):
        pl.semaphore_signal(barrier, inc=1, device_id=device, device_id_type=MESH)

    def greet_z(i, _):
        greet(at((z + i) % NZ, x, c, y))
        return 0

    lax.fori_loop(1, NZ, greet_z, 0)
    greet(at(z, x, 1 - c, y))

    def greet_handler(j, _):
        @pl.when(jnp.logical_or(j // 2 != x, handler_y(j) != y))
        def _():
            greet(at(z, j // 2, c, handler_y(j)))
        return 0

    lax.fori_loop(0, 8, greet_handler, 0)

    @pl.when(handles)
    def _():
        def greet_relay(i, _):
            @pl.when(i != xy)
            def _():
                greet(at(z, i // NY, c, i % NY))
            return 0

        lax.fori_loop(0, NX * NY, greet_relay, 0)

    wide = emb_ref[...].astype(F32)
    norm_sq = jnp.sum(wide * wide, axis=1, keepdims=True) + 1e-06
    unit[...] = (wide * lax.rsqrt(norm_sq)).astype(BF16)
    label = lab_ref[...]
    owner = label >> 3
    owner_f = jnp.broadcast_to(owner.astype(F32), (ROWS, ROWS))
    earlier = (owner_f == owner_f.T) & (iota((ROWS, ROWS), 0) < iota((ROWS, ROWS), 1))
    rank = jnp.sum(jnp.where(earlier, 1.0, 0.0), axis=0, keepdims=True).astype(jnp.int32)
    meta[0] = label * 4 + rank

    pl.semaphore_wait(barrier, jnp.where(handles, 38, 24))

    def raw_copy(way, hop, piece):
        rows = pl.ds(piece * PIECE, PIECE)
        src = unit.at[rows] if hop == 0 else raw.at[way, 0, rows]
        to = (z + (1 if way == 0 else NZ - 1)) % NZ
        return pltpu.make_async_remote_copy(
            src_ref=src, dst_ref=raw.at[way, hop, rows],
            send_sem=raw_send.at[way, hop, piece], recv_sem=raw_recv.at[way, hop, piece],
            device_id=at(to, x, c, y), device_id_type=MESH,
        )

    pieces = ROWS // PIECE
    for piece in range(pieces):
        for way in range(2):
            raw_copy(way, 0, piece).start()

    def meta_copy(pos):
        return pltpu.make_async_remote_copy(
            src_ref=meta.at[0], dst_ref=meta.at[pos],
            send_sem=meta_send.at[pos], recv_sem=meta_recv,
            device_id=at(up(pos), x, c, y), device_id_type=MESH,
        )

    def meta_start(pos, _):
        meta_copy(pos).start()
        return 0

    lax.fori_loop(1, NZ, meta_start, 0)

    def slots_of(code):
        return ((code >> 5) << 2) | (code & 3)

    def pack_near(pos, rows_ref):
        slot = slots_of(meta[pos])
        pick = one_hot(slot == z * 32 + iota((32, ROWS), 0))
        farr[pl.ds(pos * 32, 32), :] = dot_nn(pick, rows_ref[...]).astype(BF16)

    pack_near(0, unit)

    for piece in range(pieces):
        for way in range(2):
            raw_copy(way, 0, piece).wait_recv()
            raw_copy(way, 1, piece).start()

    pltpu.make_async_copy(meta.at[pl.ds(1, NZ - 1)], meta.at[pl.ds(1, NZ - 1)], meta_recv).wait()
    pack_near(1, raw.at[0, 0])
    pack_near(2, raw.at[1, 0])

    def far_copy(way, g):
        to = (z + (1 + g if way == 0 else NZ - 1 - g)) % NZ
        if g < 5:
            pos = 2 * g + 5 + way
            src, dst, sem = fsend.at[way, pl.ds(g * 32, 32)], farr.at[pl.ds(pos * 32, 32)], pos
        else:
            src = fsend.at[way, pl.ds(160 + way * 16, 16)]
            dst, sem = farr.at[pl.ds(480 + way * 16, 16)], 15 + way
        return pltpu.make_async_remote_copy(
            src_ref=src, dst_ref=dst, send_sem=far_send.at[way, g], recv_sem=far_recv.at[sem],
            device_id=at(to, x, c, y), device_id_type=MESH,
        )

    for way in range(2):
        for piece in range(pieces):
            raw_copy(way, 1, piece).wait_recv()
        slot = slots_of(meta[3 + way])
        row = iota((192, ROWS), 0)
        step = 1 + (row >> 5)
        plane = (z + (step if way == 0 else NZ - step)) & (NZ - 1)
        pick = one_hot(slot == (plane << 5) + (row & 31))
        fsend[way] = dot_nn(pick, raw[way, 1]).astype(BF16)
        for g in range(6):
            far_copy(way, g).start()

    pack_near(3, raw.at[0, 1])
    pack_near(4, raw.at[1, 1])

    def plane_dst(q):
        return own.at[pl.ds(q * 256 + pl.multiple_of(xy * 16, 16), 16)]

    def plane_copy(q, j):
        return pltpu.make_async_remote_copy(
            src_ref=psend.at[pl.ds(q * ROWS + pl.multiple_of(j * 16, 16), 16)], dst_ref=plane_dst(q),
            send_sem=plane_send.at[q, j], recv_sem=own_recv.at[q],
            device_id=at(z, j // 2, c, handler_y(j)), device_id_type=MESH,
        )

    def relay(q):
        here = pl.ds(q * ROWS, ROWS)
        i = iota((ROWS, ROWS), 0)
        lane = iota((ROWS, ROWS), 1)
        zq, j4 = (i >> 2) & 3, ((i >> 4) << 2) | (i & 3)
        order = one_hot(lane == zq * 32 + j4)
        psend[here, :D] = dot_nn(order, farr[here, :]).astype(BF16)
        same = jnp.zeros((ROWS, EXT), F32)
        for k in range(4):
            code = meta[q * 4 + k]
            pick = one_hot((slots_of(code) == z * 32 + j4) & (zq == k))
            same += dot_nt(pick, one_hot((((code >> 2) & 7) == i) | (i == 8)))
        right = jnp.where(lane < 8, PENALTY * same - PENALTY, jnp.where(lane == 8, -PENALTY * same, 0.0))
        psend[here, D:] = right.astype(BF16)

        def send(j, _):
            mine = jnp.logical_and(j // 2 == x, handler_y(j) == y)

            @pl.when(mine)
            def _():
                pltpu.make_async_copy(
                    psend.at[pl.ds(q * ROWS + pl.multiple_of(j * 16, 16), 16)], plane_dst(q), own_recv.at[q]
                ).start()

            @pl.when(jnp.logical_not(mine))
            def _():
                plane_copy(q, j).start()
            return 0

        lax.fori_loop(0, 8, send, 0)

    def sib_copy(q):
        rows = pl.ds(q * 256, 256)
        return pltpu.make_async_remote_copy(
            src_ref=own.at[rows], dst_ref=sib.at[rows], send_sem=sib_send.at[q], recv_sem=sib_recv.at[q],
            device_id=at(z, x, 1 - c, y), device_id_type=MESH,
        )

    def terms(a, right_ref, b):
        sims = dot_nt(left[pl.ds(a * 256, 256), :], right_ref[pl.ds(b * 256, 256), :])
        return jnp.exp2(sims * LOG2E10)

    def add_rows(a, e):
        rows = pl.ds(a * 256, 256)
        acc[rows, :] = acc[rows, :] + (e[:, :128] + e[:, 128:])

    def handle(q):
        @pl.when(handles)
        def _():
            rows = pl.ds(q * 256, 256)
            pltpu.make_async_copy(own.at[rows], own.at[rows], own_recv.at[q]).wait()
            sib_copy(q).start()
            left[rows, :D] = own[rows, :D]
            is_cluster = iota((256, EXT), 1) < 9
            left[rows, D:] = jnp.where(
                is_cluster, own[rows, D:].astype(F32) * (1.0 / PENALTY) + 1.0, 0.0
            ).astype(BF16)
            e = terms(q, own, q)
            acc[rows, :] = e[:, :128] + e[:, 128:]
            colacc[q] = jnp.zeros((8, 256), F32)

            def own_pair(a, _):
                e = terms(a, own, q)
                add_rows(a, e)
                colacc[q] = colacc[q] + jnp.sum(e.reshape(32, 8, 256), axis=0)
                return 0

            lax.fori_loop(0, q, own_pair, 0)
            sib_copy(q).wait_recv()

            def sib_new(a, _):
                add_rows(a, terms(a, sib, q))
                return 0

            lax.fori_loop(0, q + 1, sib_new, 0)

            def sib_old(b, _):
                add_rows(q, terms(q, sib, b))
                return 0

            lax.fori_loop(0, q, sib_old, 0)

    relay(0)
    for pos in (5, 6, 7):
        far_copy((pos - 5) % 2, (pos - 5) // 2).wait_recv()
    relay(1)
    handle(0)
    handle(1)
    for pos in (8, 9, 10, 11):
        far_copy((pos - 5) % 2, (pos - 5) // 2).wait_recv()
    relay(2)
    handle(2)
    for pos in (12, 13, 14):
        far_copy((pos - 5) % 2, (pos - 5) // 2).wait_recv()
    far_copy(0, 5).wait_recv()
    far_copy(1, 5).wait_recv()
    relay(3)
    handle(3)

    def tot_copy(i):
        return pltpu.make_async_remote_copy(
            src_ref=tot.at[i // 8], dst_ref=back.at[my_owner],
            send_sem=tot_send.at[i], recv_sem=tot_recv,
            device_id=at(z, i // NY, c, i % NY), device_id_type=MESH,
        )

    @pl.when(handles)
    def _():
        for q in range(4):
            for h in range(2):
                part = acc[pl.ds(q * 256 + h * 128, 128), :].T
                total = jnp.sum(part, axis=0, keepdims=True) + jnp.sum(
                    colacc[q, :, h * 128 : h * 128 + 128], axis=0, keepdims=True
                )
                tot[h, q : q + 1, :] = total
        tot[0, 4:8, :] = jnp.zeros((4, 128), F32)
        tot[1, 4:8, :] = jnp.zeros((4, 128), F32)

        def send(i, _):
            @pl.when(i == xy)
            def _():
                pltpu.make_async_copy(tot.at[i // 8], back.at[my_owner], tot_recv).start()

            @pl.when(i != xy)
            def _():
                tot_copy(i).start()
            return 0

        lax.fori_loop(0, NX * NY, send, 0)

    pltpu.make_async_copy(back, back, tot_recv).wait()
    for j in range(8):
        for q in range(4):
            ret[q, j : j + 1, :] = back[j, q : q + 1, :]

    def ret_copy(pos):
        return pltpu.make_async_remote_copy(
            src_ref=ret.at[pos // 4], dst_ref=wts.at[z],
            send_sem=ret_send.at[pos], recv_sem=ret_recv,
            device_id=at(down(pos), x, c, y), device_id_type=MESH,
        )

    def ret_start(pos, _):
        ret_copy(pos).start()
        return 0

    lax.fori_loop(1, NZ, ret_start, 0)
    wts[z] = ret[0]
    pltpu.make_async_copy(
        wts.at[pl.ds(0, NZ - 1)], wts.at[pl.ds(0, NZ - 1)], ret_recv
    ).wait()

    code = meta[0]
    table = wts[...].reshape(NZ * 8, 128).T
    lines = jnp.where((code >> 5) == iota((NZ * 8, ROWS), 0), 1.0, 0.0)
    picked = jnp.dot(table, lines, precision=lax.Precision.HIGHEST, preferred_element_type=F32)
    ahead = ((code >> 8) - z) & (NZ - 1)
    pos = jnp.where(ahead == 0, 0, jnp.where(ahead <= 8, 2 * ahead - 1, 2 * (NZ - ahead)))
    lane = (xy % 8) * 16 + (pos & 3) * 4 + (code & 3)
    total = jnp.sum(jnp.where(iota((128, ROWS), 0) == lane, picked, 0.0), axis=0, keepdims=True)
    out_ref[...] = 0.1 * jnp.log(total)

    for way in range(2):
        for hop in range(2):
            for piece in range(pieces):
                raw_copy(way, hop, piece).wait_send()
        for g in range(6):
            far_copy(way, g).wait_send()

    def drain_z(pos, _):
        meta_copy(pos).wait_send()
        ret_copy(pos).wait_send()
        return 0

    lax.fori_loop(1, NZ, drain_z, 0)

    def drain_plane(j, _):
        @pl.when(jnp.logical_or(j // 2 != x, handler_y(j) != y))
        def _():
            for q in range(4):
                plane_copy(q, j).wait_send()
        return 0

    lax.fori_loop(0, 8, drain_plane, 0)

    @pl.when(handles)
    def _():
        for q in range(4):
            sib_copy(q).wait_send()

        def drain_tot(i, _):
            @pl.when(i != xy)
            def _():
                tot_copy(i).wait_send()
            return 0

        lax.fori_loop(0, NX * NY, drain_tot, 0)


def per_device(embeddings, labels):
    dma = pltpu.SemaphoreType.DMA
    vmem = pltpu.VMEM
    weight = pl.pallas_call(
        kernel,
        out_shape=jax.ShapeDtypeStruct((1, ROWS), F32),
        in_specs=[pl.BlockSpec(memory_space=pltpu.VMEM)] * 2,
        out_specs=pl.BlockSpec(memory_space=pltpu.VMEM),
        scratch_shapes=[
            vmem((ROWS, D), BF16),
            vmem((2, 2, ROWS, D), BF16),
            vmem((2, 192, D), BF16),
            vmem((NZ * 32, D), BF16),
            vmem((NZ, 1, ROWS), jnp.int32),
            vmem((4 * ROWS, WIDE), BF16),
            vmem((1024, WIDE), BF16),
            vmem((1024, WIDE), BF16),
            vmem((1024, WIDE), BF16),
            vmem((1024, 128), F32),
            vmem((4, 8, 256), F32),
            vmem((2, 8, 128), F32),
            vmem((8, 8, 128), F32),
            vmem((4, 8, 128), F32),
            vmem((NZ, 8, 128), F32),
            dma((2, 2, ROWS // PIECE)), dma((2, 2, ROWS // PIECE)),
            dma((2, 6)), dma((17,)),
            dma((NZ,)), dma,
            dma((4, 8)), dma((4,)),
            dma((4,)), dma((4,)),
            dma((NX * NY,)), dma,
            dma((NZ,)), dma,
        ],
        compiler_params=pltpu.CompilerParams(
            collective_id=0, has_side_effects=True, vmem_limit_bytes=40 * 1024 * 1024
        ),
        name="soft_dedup",
    )(embeddings, labels.reshape(1, ROWS))
    return weight.reshape(ROWS)


def solution(mesh):
    placed = (P(("shard", "split"), None), P(("shard", "split")))
    return jax.shard_map(
        per_device, mesh=mesh, in_specs=placed, out_specs=P(("shard", "split")), check_vma=False
    )
```

```python
import functools

import jax
import jax.numpy as jnp
from jax import lax
from jax.experimental import pallas as pl
from jax.experimental.pallas import tpu as pltpu
from jax.sharding import PartitionSpec as P

MESH = pl.DeviceIdType.MESH
F32 = jnp.float32
BF16 = jnp.bfloat16

D = 768
EXT = 128
WIDE = D + EXT
ROWS = 128
NZ, NX, NY = 16, 4, 4
PIECE = 64
PENALTY = 16.0
LOG2E10 = 14.426950408889634


def one_hot(cond):
    return jnp.where(cond, 1.0, 0.0).astype(BF16)


def dot_nn(a, b):
    return lax.dot_general(a, b, (((1,), (0,)), ((), ())), preferred_element_type=F32)


def dot_nt(a, b):
    return lax.dot_general(a, b, (((1,), (1,)), ((), ())), preferred_element_type=F32)


def iota(shape, dim):
    return lax.broadcasted_iota(jnp.int32, shape, dim)


def kernel(
    emb_hbm, lab_hbm, out_ref,
    emb, lab, unit, raw, fsend, farr, meta, psend, pext, own, sib, left, acc, colacc, tot, back, ret, wts,
    in_sem, known, raw_send, raw_recv, far_send, far_recv, meta_send, meta_recv, plane_send, own_recv,
    ext_send, ext_recv, sib_send, sib_recv, tot_send, tot_recv, ret_send, ret_recv,
):
    p = lax.axis_index("shard")
    y = lax.axis_index("split")
    z = p // 8
    x = (p % 8) // 2
    c = p % 2
    xy = x * NY + y
    turn = (y - x + NY) % NY
    handles = turn % 2 == 0
    my_owner = x * 2 + turn // 2

    def at(zz, xx, cc, yy):
        return (zz * 8 + xx * 2 + cc, yy)

    def handler_y(j):
        return (2 * (j % 2) + j // 2) % NY

    def up(pos):
        k = (pos + 1) // 2
        return (z + jnp.where(pos % 2 == 1, k, NZ - k)) % NZ

    def down(pos):
        k = (pos + 1) // 2
        return (z + jnp.where(pos % 2 == 1, NZ - k, k)) % NZ

    barrier = pltpu.get_barrier_semaphore()
    z_by = lambda k: at((z + k + NZ) & (NZ - 1), x, c, y)
    x_by = lambda k: at(z, (x + k) & 3, c, y)
    y_by = lambda k: at(z, x, c, (y + k) & 3)
    near = [z_by(1), z_by(-1), x_by(1), x_by(3), y_by(1), y_by(3)]
    for device in near + [at(z, x, 1 - c, y)]:
        pl.semaphore_signal(barrier, inc=1, device_id=device, device_id_type=MESH)
    load_emb = pltpu.make_async_copy(emb_hbm, emb, in_sem.at[0])
    load_lab = pltpu.make_async_copy(lab_hbm, lab, in_sem.at[1])
    load_lab.start()
    load_emb.start()

    rounds = [
        near,
        [z_by(2), z_by(-2)],
        [z_by(4), z_by(-4)],
        [y_by(1), y_by(2), y_by(3)],
        [x_by(1), x_by(2), x_by(3)],
    ]

    def tell(r):
        for device in rounds[r]:
            pl.semaphore_signal(known.at[r], inc=1, device_id=device, device_id_type=MESH)

    def learn(r):
        pl.semaphore_wait(known.at[r], len(rounds[r]))

    load_lab.wait()
    load_emb.wait()
    wide = emb[...].astype(F32)
    norm_sq = jnp.sum(wide * wide, axis=1, keepdims=True) + 1e-06
    unit[...] = (wide * lax.rsqrt(norm_sq)).astype(BF16)
    label = lab[...]
    owner = label >> 3
    owner_f = jnp.broadcast_to(owner.astype(F32), (ROWS, ROWS))
    earlier = (owner_f == owner_f.T) & (iota((ROWS, ROWS), 0) < iota((ROWS, ROWS), 1))
    rank = jnp.sum(jnp.where(earlier, 1.0, 0.0), axis=0, keepdims=True).astype(jnp.int32)
    meta[0] = label * 4 + rank

    pl.semaphore_wait(barrier, 7)

    def raw_copy(way, hop, piece):
        rows = pl.ds(piece * PIECE, PIECE)
        src = unit.at[rows] if hop == 0 else raw.at[way, 0, rows]
        to = (z + (1 if way == 0 else NZ - 1)) % NZ
        return pltpu.make_async_remote_copy(
            src_ref=src, dst_ref=raw.at[way, hop, rows],
            send_sem=raw_send.at[way, hop, piece], recv_sem=raw_recv.at[way, hop, piece],
            device_id=at(to, x, c, y), device_id_type=MESH,
        )

    pieces = ROWS // PIECE
    for piece in range(pieces):
        for way in range(2):
            raw_copy(way, 0, piece).start()

    def meta_copy(pos, sem):
        return pltpu.make_async_remote_copy(
            src_ref=meta.at[0], dst_ref=meta.at[pos],
            send_sem=meta_send.at[pos], recv_sem=meta_recv.at[sem],
            device_id=at(up(pos), x, c, y), device_id_type=MESH,
        )

    meta_copy(1, 0).start()
    meta_copy(2, 0).start()
    tell(0)
    learn(0)
    meta_copy(3, 0).start()
    meta_copy(4, 0).start()
    tell(1)
    learn(1)
    tell(2)

    def slots_of(code):
        return ((code >> 5) << 2) | (code & 3)

    def pack_near(pos, rows_ref):
        slot = slots_of(meta[pos])
        pick = one_hot(slot == z * 32 + iota((32, ROWS), 0))
        farr[pl.ds(pos * 32, 32), :] = dot_nn(pick, rows_ref[...]).astype(BF16)

    def far_copy(way, g):
        step = 1 + g if g < 5 else 7
        to = (z + (step if way == 0 else NZ - step)) & (NZ - 1)
        if g < 5:
            pos = 2 * g + 5 + way
            src, dst, sem = fsend.at[way, pl.ds(g * 32, 32)], farr.at[pl.ds(pos * 32, 32)], pos
        else:
            src = fsend.at[way, pl.ds(160, 16)]
            dst, sem = farr.at[pl.ds(480 + way * 16, 16)], 15 + way
        return pltpu.make_async_remote_copy(
            src_ref=src, dst_ref=dst, send_sem=far_send.at[way, g], recv_sem=far_recv.at[sem],
            device_id=at(to, x, c, y), device_id_type=MESH,
        )

    for piece in range(pieces):
        for way in range(2):
            raw_copy(way, 0, piece).wait_recv()
            raw_copy(way, 1, piece).start()
        if piece == 0:
            learn(2)
            tell(3)
    near_meta = meta.at[pl.ds(1, 4)]
    pltpu.make_async_copy(near_meta, near_meta, meta_recv.at[0]).wait()
    for way in range(2):
        plane = (z + (7 if way == 0 else NZ - 7)) & (NZ - 1)
        pick = one_hot(slots_of(meta[1 + way]) == (plane << 5) + way * 16 + iota((16, ROWS), 0))
        fsend[way, 160:] = dot_nn(pick, raw[way, 0]).astype(BF16)
        far_copy(way, 5).start()

    def meta_start(pos, _):
        meta_copy(pos, 1).start()
        return 0

    lax.fori_loop(5, NZ, meta_start, 0)
    learn(3)
    tell(4)
    pack_near(0, unit)
    pack_near(1, raw.at[0, 0])
    pack_near(2, raw.at[1, 0])

    for way in range(2):
        for piece in range(pieces):
            raw_copy(way, 1, piece).wait_recv()
        slot = slots_of(meta[3 + way])
        row = iota((160, ROWS), 0)
        step = 1 + (row >> 5)
        plane = (z + (step if way == 0 else NZ - step)) & (NZ - 1)
        pick = one_hot(slot == (plane << 5) + (row & 31))
        fsend[way, :160] = dot_nn(pick, raw[way, 1]).astype(BF16)
        for g in range(5):
            far_copy(way, g).start()

    pack_near(3, raw.at[0, 1])
    pack_near(4, raw.at[1, 1])
    learn(4)

    i128 = iota((ROWS, ROWS), 0)
    lane = iota((ROWS, ROWS), 1)
    zq, j4 = (i128 >> 2) & 3, ((i128 >> 4) << 2) | (i128 & 3)

    def is_here(j):
        return jnp.logical_and(j // 2 == x, handler_y(j) == y)

    def mine16():
        return pl.ds(pl.multiple_of(xy * 16, 16), 16)

    def ext_copy(j):
        return pltpu.make_async_remote_copy(
            src_ref=pext.at[j], dst_ref=own.at[:, mine16(), pl.ds(D, EXT)],
            send_sem=ext_send.at[j], recv_sem=ext_recv,
            device_id=at(z, j // 2, c, handler_y(j)), device_id_type=MESH,
        )

    def plane_src(q, j):
        return psend.at[pl.ds(q * ROWS + pl.multiple_of(j * 16, 16), 16)]

    def plane_copy(q, j):
        return pltpu.make_async_remote_copy(
            src_ref=plane_src(q, j), dst_ref=own.at[q, mine16(), pl.ds(0, D)],
            send_sem=plane_send.at[q, j], recv_sem=own_recv.at[q, x],
            device_id=at(z, j // 2, c, handler_y(j)), device_id_type=MESH,
        )

    far_meta = meta.at[pl.ds(5, NZ - 5)]
    pltpu.make_async_copy(far_meta, far_meta, meta_recv.at[1]).wait()
    for q in range(4):
        same = jnp.zeros((ROWS, EXT), F32)
        for k in range(4):
            code = meta[q * 4 + k]
            pick = one_hot((slots_of(code) == z * 32 + j4) & (zq == k))
            same += dot_nt(pick, one_hot((((code >> 2) & 7) == i128) | (i128 == 8)))
        right = jnp.where(lane < 8, PENALTY * same - PENALTY, jnp.where(lane == 8, -PENALTY * same, 0.0))
        pext[:, q] = right.astype(BF16).reshape(8, 16, EXT)

    def ext_start(j, _):
        @pl.when(is_here(j))
        def _():
            pltpu.make_async_copy(pext.at[j], own.at[:, mine16(), pl.ds(D, EXT)], ext_recv).start()

        @pl.when(jnp.logical_not(is_here(j)))
        def _():
            ext_copy(j).start()
        return 0

    lax.fori_loop(0, 8, ext_start, 0)

    def relay(q):
        here = pl.ds(q * ROWS, ROWS)
        order = one_hot(lane == zq * 32 + j4)
        psend[here, :] = dot_nn(order, farr[here, :]).astype(BF16)

        def send(j, _):
            @pl.when(is_here(j))
            def _():
                pltpu.make_async_copy(
                    plane_src(q, j), own.at[q, mine16(), pl.ds(0, D)], own_recv.at[q, x]
                ).start()

            @pl.when(jnp.logical_not(is_here(j)))
            def _():
                plane_copy(q, j).start()
            return 0

        lax.fori_loop(0, 8, send, 0)

    def sib_copy(q, g):
        rows = pl.ds(pl.multiple_of(g * 64, 64), 64)
        return pltpu.make_async_remote_copy(
            src_ref=own.at[q, rows], dst_ref=sib.at[q, rows],
            send_sem=sib_send.at[q, g], recv_sem=sib_recv.at[q, g],
            device_id=at(z, x, 1 - c, y), device_id_type=MESH,
        )

    def terms(left_rows, right_rows):
        return jnp.exp2(dot_nt(left_rows, right_rows) * LOG2E10)

    def lane_sums(e):
        total = e[:, :128]
        for k in range(1, e.shape[1] // 128):
            total = total + e[:, k * 128 : k * 128 + 128]
        return total

    def handle(q):
        @pl.when(handles)
        def _():
            old, new = q * 256, q * 256 + 256
            if q == 0:
                lanes = own.at[:, :, pl.ds(D, EXT)]
                pltpu.make_async_copy(lanes, lanes, ext_recv).wait()

            def take(k, _):
                g = (x + k) & 3
                rows = own.at[q, pl.ds(pl.multiple_of(g * 64, 64), 64), pl.ds(0, D)]
                pltpu.make_async_copy(rows, rows, own_recv.at[q, g]).wait()
                sib_copy(q, g).start()
                return 0

            lax.fori_loop(0, 4, take, 0)
            left[old:new, :D] = own[q, :, :D]
            is_cluster = iota((256, EXT), 1) < 9
            left[old:new, D:] = jnp.where(
                is_cluster, own[q, :, D:].astype(F32) * (1.0 / PENALTY) + 1.0, 0.0
            ).astype(BF16)
            e = terms(left[:new, :], own[q])
            sums = lane_sums(e)
            acc[old:new, :] = sums[old:]
            if q:
                acc[:old, :] = acc[:old, :] + sums[:old]
                colacc[q] = jnp.sum(e[:old].reshape(old // 8, 8, 256), axis=0)
            else:
                colacc[q] = jnp.zeros((8, 256), F32)

            def sib_wait(g, _):
                sib_copy(q, g).wait_recv()
                return 0

            lax.fori_loop(0, 4, sib_wait, 0)
            acc[:new, :] = acc[:new, :] + lane_sums(terms(left[:new, :], sib[q]))
            if q:
                e = terms(left[old:new, :], sib[:q].reshape(old, WIDE))
                acc[old:new, :] = acc[old:new, :] + lane_sums(e)

    relay(0)
    for pos in (5, 6, 7):
        far_copy((pos - 5) % 2, (pos - 5) // 2).wait_recv()
    relay(1)
    handle(0)
    handle(1)
    for pos in (8, 9, 10, 11):
        far_copy((pos - 5) % 2, (pos - 5) // 2).wait_recv()
    relay(2)
    handle(2)
    for pos in (12, 13, 14):
        far_copy((pos - 5) % 2, (pos - 5) // 2).wait_recv()
    far_copy(0, 5).wait_recv()
    far_copy(1, 5).wait_recv()
    relay(3)
    handle(3)

    def tot_copy(i):
        return pltpu.make_async_remote_copy(
            src_ref=tot.at[i // 8], dst_ref=back.at[my_owner],
            send_sem=tot_send.at[i], recv_sem=tot_recv,
            device_id=at(z, i // NY, c, i % NY), device_id_type=MESH,
        )

    @pl.when(handles)
    def _():
        for q in range(4):
            for h in range(2):
                part = acc[pl.ds(q * 256 + h * 128, 128), :].T
                total = jnp.sum(part, axis=0, keepdims=True) + jnp.sum(
                    colacc[q, :, h * 128 : h * 128 + 128], axis=0, keepdims=True
                )
                tot[h, q : q + 1, :] = total
        tot[0, 4:8, :] = jnp.zeros((4, 128), F32)
        tot[1, 4:8, :] = jnp.zeros((4, 128), F32)

        def send(i, _):
            @pl.when(i == xy)
            def _():
                pltpu.make_async_copy(tot.at[i // 8], back.at[my_owner], tot_recv).start()

            @pl.when(i != xy)
            def _():
                tot_copy(i).start()
            return 0

        lax.fori_loop(0, NX * NY, send, 0)

    pltpu.make_async_copy(back, back, tot_recv).wait()
    for j in range(8):
        for q in range(4):
            ret[q, j : j + 1, :] = back[j, q : q + 1, :]

    def ret_copy(pos):
        return pltpu.make_async_remote_copy(
            src_ref=ret.at[pos // 4], dst_ref=wts.at[z],
            send_sem=ret_send.at[pos], recv_sem=ret_recv,
            device_id=at(down(pos), x, c, y), device_id_type=MESH,
        )

    def ret_start(pos, _):
        ret_copy(pos).start()
        return 0

    lax.fori_loop(1, NZ, ret_start, 0)
    wts[z] = ret[0]
    pltpu.make_async_copy(
        wts.at[pl.ds(0, NZ - 1)], wts.at[pl.ds(0, NZ - 1)], ret_recv
    ).wait()

    code = meta[0]
    table = wts[...].reshape(NZ * 8, 128).T
    lines = jnp.where((code >> 5) == iota((NZ * 8, ROWS), 0), 1.0, 0.0)
    picked = jnp.dot(table, lines, precision=lax.Precision.HIGHEST, preferred_element_type=F32)
    ahead = ((code >> 8) - z) & (NZ - 1)
    pos = jnp.where(ahead == 0, 0, jnp.where(ahead <= 8, 2 * ahead - 1, 2 * (NZ - ahead)))
    lane = (xy % 8) * 16 + (pos & 3) * 4 + (code & 3)
    total = jnp.sum(jnp.where(iota((128, ROWS), 0) == lane, picked, 0.0), axis=0, keepdims=True)
    out_ref[...] = 0.1 * jnp.log(total)

    for way in range(2):
        for hop in range(2):
            for piece in range(pieces):
                raw_copy(way, hop, piece).wait_send()
        for g in range(6):
            far_copy(way, g).wait_send()

    def drain_z(pos, _):
        meta_copy(pos, 0).wait_send()
        ret_copy(pos).wait_send()
        return 0

    lax.fori_loop(1, NZ, drain_z, 0)

    def drain_plane(j, _):
        @pl.when(jnp.logical_not(is_here(j)))
        def _():
            ext_copy(j).wait_send()
            for q in range(4):
                plane_copy(q, j).wait_send()
        return 0

    lax.fori_loop(0, 8, drain_plane, 0)

    @pl.when(handles)
    def _():
        def drain_sib(k, _):
            sib_copy(k >> 2, k & 3).wait_send()
            return 0

        lax.fori_loop(0, 16, drain_sib, 0)

        def drain_tot(i, _):
            @pl.when(i != xy)
            def _():
                tot_copy(i).wait_send()
            return 0

        lax.fori_loop(0, NX * NY, drain_tot, 0)


def per_device(embeddings, labels):
    dma = pltpu.SemaphoreType.DMA
    vmem = pltpu.VMEM
    weight = pl.pallas_call(
        kernel,
        out_shape=jax.ShapeDtypeStruct((1, ROWS), F32),
        in_specs=[pl.BlockSpec(memory_space=pl.ANY)] * 2,
        out_specs=pl.BlockSpec(memory_space=pltpu.VMEM),
        scratch_shapes=[
            vmem((ROWS, D), BF16),
            vmem((1, ROWS), jnp.int32),
            vmem((ROWS, D), BF16),
            vmem((2, 2, ROWS, D), BF16),
            vmem((2, 176, D), BF16),
            vmem((NZ * 32, D), BF16),
            vmem((NZ, 1, ROWS), jnp.int32),
            vmem((4 * ROWS, D), BF16),
            vmem((8, 4, 16, EXT), BF16),
            vmem((4, 256, WIDE), BF16),
            vmem((4, 256, WIDE), BF16),
            vmem((1024, WIDE), BF16),
            vmem((1024, 128), F32),
            vmem((4, 8, 256), F32),
            vmem((2, 8, 128), F32),
            vmem((8, 8, 128), F32),
            vmem((4, 8, 128), F32),
            vmem((NZ, 8, 128), F32),
            dma((2,)), pltpu.SemaphoreType.REGULAR((5,)),
            dma((2, 2, ROWS // PIECE)), dma((2, 2, ROWS // PIECE)),
            dma((2, 6)), dma((17,)),
            dma((NZ,)), dma((2,)),
            dma((4, 8)), dma((4, 4)),
            dma((8,)), dma,
            dma((4, 4)), dma((4, 4)),
            dma((NX * NY,)), dma,
            dma((NZ,)), dma,
        ],
        compiler_params=pltpu.CompilerParams(
            collective_id=0, has_side_effects=True, vmem_limit_bytes=40 * 1024 * 1024
        ),
        name="soft_dedup",
    )(embeddings, labels.reshape(1, ROWS))
    return weight.reshape(ROWS)


def solution(mesh):
    placed = (P(("shard", "split"), None), P(("shard", "split")))
    return jax.shard_map(
        per_device, mesh=mesh, in_specs=placed, out_specs=P(("shard", "split")), check_vma=False
    )
```

```python
import functools

import jax
import jax.numpy as jnp
from jax import lax
from jax.experimental import pallas as pl
from jax.experimental.pallas import tpu as pltpu
from jax.sharding import PartitionSpec as P

MESH = pl.DeviceIdType.MESH
F32 = jnp.float32
BF16 = jnp.bfloat16

D = 768
EXT = 128
WIDE = D + EXT
ROWS = 128
NZ, NX, NY = 16, 4, 4
PIECE = 64
PENALTY = 16.0
LOG2E10 = 14.426950408889634


def one_hot(cond):
    return jnp.where(cond, 1.0, 0.0).astype(BF16)


def dot_nn(a, b):
    return lax.dot_general(a, b, (((1,), (0,)), ((), ())), preferred_element_type=F32)


def dot_nt(a, b):
    return lax.dot_general(a, b, (((1,), (1,)), ((), ())), preferred_element_type=F32)


def iota(shape, dim):
    return lax.broadcasted_iota(jnp.int32, shape, dim)


def kernel(
    emb_hbm, lab_hbm, out_ref,
    emb, lab, unit, raw, meta, near_out, far_out, opp_out, blocks, pext, ext_in, own, sib, left, acc, colacc,
    tot, back, ret, wts,
    in_sem, known, raw_send, raw_recv, near_send, far_send, opp_send, meta_send, meta_recv, own_recv,
    ext_send, ext_recv, sib_send, sib_recv, tot_send, tot_recv, ret_send, ret_recv,
):
    p = lax.axis_index("shard")
    y = lax.axis_index("split")
    z = p // 8
    x = (p % 8) // 2
    c = p % 2
    xy = x * NY + y
    turn = (y - x + NY) % NY
    handles = turn % 2 == 0
    my_owner = x * 2 + turn // 2

    def at(zz, xx, cc, yy):
        return (zz * 8 + xx * 2 + cc, yy)

    def handler_y(j):
        return (2 * (j % 2) + j // 2) % NY

    def up(pos):
        k = (pos + 1) // 2
        return (z + jnp.where(pos % 2 == 1, k, NZ - k)) % NZ

    def down(pos):
        k = (pos + 1) // 2
        return (z + jnp.where(pos % 2 == 1, NZ - k, k)) % NZ

    barrier = pltpu.get_barrier_semaphore()
    z_by = lambda k: at((z + k + NZ) & (NZ - 1), x, c, y)
    x_by = lambda k: at(z, (x + k) & 3, c, y)
    y_by = lambda k: at(z, x, c, (y + k) & 3)
    near = [z_by(1), z_by(-1), x_by(1), x_by(3), y_by(1), y_by(3)]
    for device in near + [at(z, x, 1 - c, y)]:
        pl.semaphore_signal(barrier, inc=1, device_id=device, device_id_type=MESH)
    load_emb = pltpu.make_async_copy(emb_hbm, emb, in_sem.at[0])
    load_lab = pltpu.make_async_copy(lab_hbm, lab, in_sem.at[1])
    load_lab.start()
    load_emb.start()

    rounds = [
        near,
        [z_by(2), z_by(-2)],
        [z_by(4), z_by(-4)],
        [y_by(1), y_by(2), y_by(3)],
        [x_by(1), x_by(2), x_by(3)],
    ]

    def tell(r):
        for device in rounds[r]:
            pl.semaphore_signal(known.at[r], inc=1, device_id=device, device_id_type=MESH)

    def learn(r):
        pl.semaphore_wait(known.at[r], len(rounds[r]))

    load_lab.wait()
    load_emb.wait()
    wide = emb[...].astype(F32)
    norm_sq = jnp.sum(wide * wide, axis=1, keepdims=True) + 1e-06
    unit[...] = (wide * lax.rsqrt(norm_sq)).astype(BF16)
    label = lab[...]
    owner = label >> 3
    owner_f = jnp.broadcast_to(owner.astype(F32), (ROWS, ROWS))
    earlier = (owner_f == owner_f.T) & (iota((ROWS, ROWS), 0) < iota((ROWS, ROWS), 1))
    rank = jnp.sum(jnp.where(earlier, 1.0, 0.0), axis=0, keepdims=True).astype(jnp.int32)
    meta[0] = label * 4 + rank

    pl.semaphore_wait(barrier, 7)

    def raw_copy(way, hop, piece):
        rows = pl.ds(piece * PIECE, PIECE)
        src = unit.at[rows] if hop == 0 else raw.at[way, 0, rows]
        to = (z + (1 if way == 0 else NZ - 1)) % NZ
        return pltpu.make_async_remote_copy(
            src_ref=src, dst_ref=raw.at[way, hop, rows],
            send_sem=raw_send.at[way, hop, piece], recv_sem=raw_recv.at[way, hop, piece],
            device_id=at(to, x, c, y), device_id_type=MESH,
        )

    pieces = ROWS // PIECE
    for piece in range(pieces):
        for way in range(2):
            raw_copy(way, 0, piece).start()

    def meta_copy(pos, sem):
        return pltpu.make_async_remote_copy(
            src_ref=meta.at[0], dst_ref=meta.at[pos],
            send_sem=meta_send.at[pos], recv_sem=meta_recv.at[sem],
            device_id=at(up(pos), x, c, y), device_id_type=MESH,
        )

    meta_copy(1, 0).start()
    meta_copy(2, 0).start()
    tell(0)
    learn(0)
    meta_copy(3, 0).start()
    meta_copy(4, 0).start()
    tell(1)
    learn(1)
    tell(2)

    def slots_of(code):
        return ((code >> 5) << 2) | (code & 3)

    def to_blocks(code, first, count, rows):
        line = iota((8 * count, ROWS), 0)
        pick = one_hot(slots_of(code) == ((first(line >> 3) << 2) | (line & 3)))
        twice = dot_nn(pick, rows)
        upper = (iota((8 * count, 128), 0) & 4) == 0
        thirds = [
            jnp.where(upper, twice[:, k : k + 128], twice[:, k + 128 : k + 256]).reshape(count, 8, 128)
            for k in range(0, D, 256)
        ]
        return jnp.concatenate(thirds, axis=1).astype(BF16)

    def is_here(j):
        return jnp.logical_and(j // 2 == x, handler_y(j) == y)

    def handler(zz, j):
        return at(zz, j // 2, c, handler_y(j))

    def block_copy(src, pos, zz, j, sem):
        return pltpu.make_async_remote_copy(
            src_ref=src, dst_ref=blocks.at[pos, xy], send_sem=sem, recv_sem=own_recv.at[pos],
            device_id=handler(zz, j), device_id_type=MESH,
        )

    def near_copy(pos, j):
        return block_copy(near_out.at[pos, j], pos, z, j, near_send.at[pos, j])

    def far_plane(way, g):
        return (z + (1 + g if way == 0 else NZ - 1 - g)) & (NZ - 1)

    def far_copy(way, g, j):
        return block_copy(far_out.at[way, g * 8 + j], 2 * g + 5 + way, far_plane(way, g), j, far_send.at[way])

    def opp_copy(way, j):
        zz = (z + (7 if way == 0 else NZ - 7)) & (NZ - 1)
        return block_copy(opp_out.at[way, j], 15, zz, way * 4 + j, opp_send.at[way])

    def send_near(pos, rows_ref):
        near_out[pos] = to_blocks(meta[pos], lambda j: z * 8 + j, 8, rows_ref[...])

        def send(j, _):
            @pl.when(is_here(j))
            def _():
                pltpu.make_async_copy(near_out.at[pos, j], blocks.at[pos, xy], own_recv.at[pos]).start()

            @pl.when(jnp.logical_not(is_here(j)))
            def _():
                near_copy(pos, j).start()
            return 0

        lax.fori_loop(0, 8, send, 0)

    for piece in range(pieces):
        for way in range(2):
            raw_copy(way, 0, piece).wait_recv()
            raw_copy(way, 1, piece).start()
        if piece == 0:
            learn(2)
            tell(3)
    near_meta = meta.at[pl.ds(1, 4)]
    pltpu.make_async_copy(near_meta, near_meta, meta_recv.at[0]).wait()
    learn(3)
    tell(4)

    def meta_start(pos, _):
        meta_copy(pos, 1).start()
        return 0

    lax.fori_loop(5, NZ, meta_start, 0)
    for way in range(2):
        zz = (z + (7 if way == 0 else NZ - 7)) & (NZ - 1)
        first = functools.partial(lambda base, j: base + j, zz * 8 + way * 4)
        opp_out[way] = to_blocks(meta[1 + way], first, 4, raw[way, 0])
    learn(4)
    for way in range(2):
        for j in range(4):
            opp_copy(way, j).start()
    send_near(0, unit)

    for way in range(2):
        for piece in range(pieces):
            raw_copy(way, 1, piece).wait_recv()

        def first(i, way=way):
            step = 1 + (i >> 3)
            return (((z + (step if way == 0 else NZ - step)) & (NZ - 1)) << 3) + (i & 7)

        far_out[way] = to_blocks(meta[3 + way], first, 40, raw[way, 1])
    for g in range(5):
        for way in range(2):
            def far_start(j, _, g=g, way=way):
                far_copy(way, g, j).start()
                return 0

            lax.fori_loop(0, 8, far_start, 0)
    send_near(1, raw.at[0, 0])
    send_near(2, raw.at[1, 0])
    send_near(3, raw.at[0, 1])
    send_near(4, raw.at[1, 1])

    i128 = iota((ROWS, ROWS), 0)
    lane = iota((ROWS, ROWS), 1)
    zq, j4 = (i128 >> 2) & 3, ((i128 >> 4) << 2) | (i128 & 3)

    def mine16():
        return pl.ds(pl.multiple_of(xy * 16, 16), 16)

    def ext_copy(j):
        return pltpu.make_async_remote_copy(
            src_ref=pext.at[j], dst_ref=ext_in.at[:, mine16()],
            send_sem=ext_send.at[j], recv_sem=ext_recv,
            device_id=at(z, j // 2, c, handler_y(j)), device_id_type=MESH,
        )

    far_meta = meta.at[pl.ds(5, NZ - 5)]
    pltpu.make_async_copy(far_meta, far_meta, meta_recv.at[1]).wait()
    for q in range(4):
        same = jnp.zeros((ROWS, EXT), F32)
        for k in range(4):
            code = meta[q * 4 + k]
            pick = one_hot((slots_of(code) == z * 32 + j4) & (zq == k))
            same += dot_nt(pick, one_hot((((code >> 2) & 7) == i128) | (i128 == 8)))
        right = jnp.where(lane < 8, PENALTY * same - PENALTY, jnp.where(lane == 8, -PENALTY * same, 0.0))
        pext[:, q] = right.astype(BF16).reshape(8, 16, EXT)

    def ext_start(j, _):
        @pl.when(is_here(j))
        def _():
            pltpu.make_async_copy(pext.at[j], ext_in.at[:, mine16()], ext_recv).start()

        @pl.when(jnp.logical_not(is_here(j)))
        def _():
            ext_copy(j).start()
        return 0

    lax.fori_loop(0, 8, ext_start, 0)

    def sib_copy(q, g):
        rows = pl.ds(pl.multiple_of(g * 64, 64), 64)
        return pltpu.make_async_remote_copy(
            src_ref=own.at[q, rows], dst_ref=sib.at[q, rows],
            send_sem=sib_send.at[q, g], recv_sem=sib_recv.at[q, g],
            device_id=at(z, x, 1 - c, y), device_id_type=MESH,
        )

    def terms(left_rows, right_rows):
        return jnp.exp2(dot_nt(left_rows, right_rows) * LOG2E10)

    def lane_sums(e):
        total = e[:, :128]
        for k in range(1, e.shape[1] // 128):
            total = total + e[:, k * 128 : k * 128 + 128]
        return total

    def handle(q):
        @pl.when(handles)
        def _():
            old, new = q * 256, q * 256 + 256
            if q == 0:
                pltpu.make_async_copy(ext_in, ext_in, ext_recv).wait()
                row, col = iota((256, 256), 0), iota((256, 256), 1)
                order = one_hot(col == (((row >> 2) & 15) << 4) + ((row >> 6) << 2) + (row & 3))
                for k in range(4):
                    own[k, :, D:] = dot_nn(order, ext_in[k]).astype(BF16)

            row, col = iota((384, 384), 0), iota((384, 384), 1)
            line = ((row >> 2) & 15) * 24 + ((row >> 6) << 2) + (row & 3)
            unpack = one_hot(col == line)

            def take(k, _):
                pos = q * 4 + k
                pltpu.make_async_copy(blocks.at[pos], blocks.at[pos], own_recv.at[pos]).wait()
                lines = blocks[pos].astype(F32).reshape(384, 128).astype(BF16)
                parts = dot_nn(unpack, lines).astype(BF16)
                here = pl.ds(pl.multiple_of(k * 64, 64), 64)
                for i in range(6):
                    own[q, here, i * 128 : i * 128 + 128] = parts[i * 64 : i * 64 + 64]
                sib_copy(q, k).start()
                return 0

            lax.fori_loop(0, 4, take, 0)
            left[old:new, :D] = own[q, :, :D]
            is_cluster = iota((256, EXT), 1) < 9
            left[old:new, D:] = jnp.where(
                is_cluster, own[q, :, D:].astype(F32) * (1.0 / PENALTY) + 1.0, 0.0
            ).astype(BF16)
            e = terms(left[:new, :], own[q])
            sums = lane_sums(e)
            acc[old:new, :] = sums[old:]
            if q:
                acc[:old, :] = acc[:old, :] + sums[:old]
                colacc[q] = jnp.sum(e[:old].reshape(old // 8, 8, 256), axis=0)
            else:
                colacc[q] = jnp.zeros((8, 256), F32)

            def sib_wait(g, _):
                sib_copy(q, g).wait_recv()
                return 0

            lax.fori_loop(0, 4, sib_wait, 0)
            acc[:new, :] = acc[:new, :] + lane_sums(terms(left[:new, :], sib[q]))
            if q:
                e = terms(left[old:new, :], sib[:q].reshape(old, WIDE))
                acc[old:new, :] = acc[old:new, :] + lane_sums(e)

    for q in range(4):
        handle(q)

    def tot_copy(i):
        return pltpu.make_async_remote_copy(
            src_ref=tot, dst_ref=back.at[my_owner],
            send_sem=tot_send.at[i], recv_sem=tot_recv,
            device_id=at(z, i // NY, c, i % NY), device_id_type=MESH,
        )

    @pl.when(handles)
    def _():
        for q in range(4):
            for h in range(2):
                part = acc[pl.ds(q * 256 + h * 128, 128), :].T
                total = jnp.sum(part, axis=0, keepdims=True) + jnp.sum(
                    colacc[q, :, h * 128 : h * 128 + 128], axis=0, keepdims=True
                )
                tot[q * 2 + h : q * 2 + h + 1, :] = total

        def send(i, _):
            @pl.when(i == xy)
            def _():
                pltpu.make_async_copy(tot, back.at[my_owner], tot_recv).start()

            @pl.when(i != xy)
            def _():
                tot_copy(i).start()
            return 0

        lax.fori_loop(0, NX * NY, send, 0)

    pltpu.make_async_copy(back, back, tot_recv).wait()
    for j in range(8):
        for k in range(8):
            ret[k, j : j + 1, :] = back[j, k : k + 1, :]

    def ret_copy(pos):
        return pltpu.make_async_remote_copy(
            src_ref=ret.at[pos // 2], dst_ref=wts.at[z],
            send_sem=ret_send.at[pos], recv_sem=ret_recv,
            device_id=at(down(pos), x, c, y), device_id_type=MESH,
        )

    def ret_start(pos, _):
        ret_copy(pos).start()
        return 0

    lax.fori_loop(1, NZ, ret_start, 0)
    wts[z] = ret[0]
    pltpu.make_async_copy(
        wts.at[pl.ds(0, NZ - 1)], wts.at[pl.ds(0, NZ - 1)], ret_recv
    ).wait()

    code = meta[0]
    table = wts[...].reshape(NZ * 8, 128).T
    lines = jnp.where((code >> 5) == iota((NZ * 8, ROWS), 0), 1.0, 0.0)
    picked = jnp.dot(table, lines, precision=lax.Precision.HIGHEST, preferred_element_type=F32)
    ahead = ((code >> 8) - z) & (NZ - 1)
    pos = jnp.where(ahead == 0, 0, jnp.where(ahead <= 8, 2 * ahead - 1, 2 * (NZ - ahead)))
    lane = (pos & 1) * 64 + xy * 4 + (code & 3)
    total = jnp.sum(jnp.where(iota((128, ROWS), 0) == lane, picked, 0.0), axis=0, keepdims=True)
    out_ref[...] = 0.1 * jnp.log(total)

    for way in range(2):
        for hop in range(2):
            for piece in range(pieces):
                raw_copy(way, hop, piece).wait_send()
        pltpu.make_async_copy(far_out.at[way], far_out.at[way], far_send.at[way]).wait()
        pltpu.make_async_copy(opp_out.at[way], opp_out.at[way], opp_send.at[way]).wait()

    def drain_z(pos, _):
        meta_copy(pos, 0).wait_send()
        ret_copy(pos).wait_send()
        return 0

    lax.fori_loop(1, NZ, drain_z, 0)

    def drain_plane(j, _):
        @pl.when(jnp.logical_not(is_here(j)))
        def _():
            ext_copy(j).wait_send()
            for pos in range(5):
                near_copy(pos, j).wait_send()
        return 0

    lax.fori_loop(0, 8, drain_plane, 0)

    @pl.when(handles)
    def _():
        def drain_sib(k, _):
            sib_copy(k >> 2, k & 3).wait_send()
            return 0

        lax.fori_loop(0, 16, drain_sib, 0)

        def drain_tot(i, _):
            @pl.when(i != xy)
            def _():
                tot_copy(i).wait_send()
            return 0

        lax.fori_loop(0, NX * NY, drain_tot, 0)


def per_device(embeddings, labels):
    dma = pltpu.SemaphoreType.DMA
    vmem = pltpu.VMEM
    weight = pl.pallas_call(
        kernel,
        out_shape=jax.ShapeDtypeStruct((1, ROWS), F32),
        in_specs=[pl.BlockSpec(memory_space=pltpu.HBM)] * 2,
        out_specs=pl.BlockSpec(memory_space=pltpu.VMEM),
        scratch_shapes=[
            vmem((ROWS, D), BF16),
            vmem((1, ROWS), jnp.int32),
            vmem((ROWS, D), BF16),
            vmem((2, 2, ROWS, D), BF16),
            vmem((NZ, 1, ROWS), jnp.int32),
            vmem((5, 8, 24, 128), BF16),
            vmem((2, 40, 24, 128), BF16),
            vmem((2, 4, 24, 128), BF16),
            vmem((NZ, 16, 24, 128), BF16),
            vmem((8, 4, 16, EXT), BF16),
            vmem((4, 256, EXT), BF16),
            vmem((4, 256, WIDE), BF16),
            vmem((4, 256, WIDE), BF16),
            vmem((1024, WIDE), BF16),
            vmem((1024, 128), F32),
            vmem((4, 8, 256), F32),
            vmem((8, 128), F32),
            vmem((8, 8, 128), F32),
            vmem((8, 8, 128), F32),
            vmem((NZ, 8, 128), F32),
            dma((2,)), pltpu.SemaphoreType.REGULAR((5,)),
            dma((2, 2, ROWS // PIECE)), dma((2, 2, ROWS // PIECE)),
            dma((5, 8)), dma((2,)), dma((2,)),
            dma((NZ,)), dma((2,)),
            dma((NZ,)),
            dma((8,)), dma,
            dma((4, 4)), dma((4, 4)),
            dma((NX * NY,)), dma,
            dma((NZ,)), dma,
        ],
        compiler_params=pltpu.CompilerParams(
            collective_id=0, has_side_effects=True, vmem_limit_bytes=40 * 1024 * 1024
        ),
        name="soft_dedup",
    )(embeddings, labels.reshape(1, ROWS))
    return weight.reshape(ROWS)


def solution(mesh):
    placed = (P(("shard", "split"), None), P(("shard", "split")))
    return jax.shard_map(
        per_device, mesh=mesh, in_specs=placed, out_specs=P(("shard", "split")), check_vma=False
    )
```

```python
import functools

import jax
import jax.numpy as jnp
from jax import lax
from jax.experimental import pallas as pl
from jax.experimental.pallas import tpu as pltpu
from jax.sharding import PartitionSpec as P

MESH = pl.DeviceIdType.MESH
F32 = jnp.float32
BF16 = jnp.bfloat16

D = 768
EXT = 128
WIDE = D + EXT
ROWS = 128
NZ, NX, NY = 16, 4, 4
PIECE = 64
PENALTY = 16.0
LOG2E10 = 14.426950408889634


def one_hot(cond):
    return jnp.where(cond, 1.0, 0.0).astype(BF16)


def dot_nn(a, b):
    return lax.dot_general(a, b, (((1,), (0,)), ((), ())), preferred_element_type=F32)


def dot_nt(a, b):
    return lax.dot_general(a, b, (((1,), (1,)), ((), ())), preferred_element_type=F32)


def iota(shape, dim):
    return lax.broadcasted_iota(jnp.int32, shape, dim)


def kernel(
    emb_hbm, lab_hbm, out_ref,
    emb, lab, unit, raw, meta, near_out, far_out, opp_out, blocks, pext, ext_in, own, sib, left, acc, colacc,
    tot, back, ret, wts,
    in_sem, known, raw_send, raw_recv, near_send, far_send, opp_send, meta_send, meta_recv, own_recv,
    ext_send, ext_recv, sib_send, sib_recv, tot_send, tot_recv, ret_send, ret_recv,
):
    p = lax.axis_index("shard")
    y = lax.axis_index("split")
    z = p // 8
    x = (p % 8) // 2
    c = p % 2
    xy = x * NY + y
    turn = (y - x + NY) % NY
    handles = turn % 2 == 0
    my_owner = x * 2 + turn // 2

    def at(zz, xx, cc, yy):
        return (zz * 8 + xx * 2 + cc, yy)

    def handler_y(j):
        return (2 * (j % 2) + j // 2) % NY

    def up(pos):
        k = (pos + 1) // 2
        return (z + jnp.where(pos % 2 == 1, k, NZ - k)) % NZ

    def down(pos):
        k = (pos + 1) // 2
        return (z + jnp.where(pos % 2 == 1, NZ - k, k)) % NZ

    barrier = pltpu.get_barrier_semaphore()
    z_by = lambda k: at((z + k + NZ) & (NZ - 1), x, c, y)
    x_by = lambda k: at(z, (x + k) & 3, c, y)
    y_by = lambda k: at(z, x, c, (y + k) & 3)
    near = [z_by(1), z_by(-1), x_by(1), x_by(3), y_by(1), y_by(3)]
    for device in near + [at(z, x, 1 - c, y)]:
        pl.semaphore_signal(barrier, inc=1, device_id=device, device_id_type=MESH)
    load_emb = pltpu.make_async_copy(emb_hbm, emb, in_sem.at[0])
    load_lab = pltpu.make_async_copy(lab_hbm, lab, in_sem.at[1])
    load_lab.start()
    load_emb.start()

    rounds = [
        near,
        [z_by(2), z_by(-2)],
        [z_by(4), z_by(-4)],
        [y_by(1), y_by(2), y_by(3)],
        [x_by(1), x_by(2), x_by(3)],
    ]

    def tell(r):
        for device in rounds[r]:
            pl.semaphore_signal(known.at[r], inc=1, device_id=device, device_id_type=MESH)

    def learn(r):
        pl.semaphore_wait(known.at[r], len(rounds[r]))

    load_lab.wait()
    load_emb.wait()
    wide = emb[...].astype(F32)
    norm_sq = jnp.sum(wide * wide, axis=1, keepdims=True) + 1e-06
    unit[...] = (wide * lax.rsqrt(norm_sq)).astype(BF16)
    label = lab[...]
    owner = label >> 3
    owner_f = jnp.broadcast_to(owner.astype(F32), (ROWS, ROWS))
    earlier = (owner_f == owner_f.T) & (iota((ROWS, ROWS), 0) < iota((ROWS, ROWS), 1))
    rank = jnp.sum(jnp.where(earlier, 1.0, 0.0), axis=0, keepdims=True).astype(jnp.int32)
    meta[0] = label * 4 + rank

    pl.semaphore_wait(barrier, 7)

    def raw_copy(way, hop, piece):
        rows = pl.ds(piece * PIECE, PIECE)
        src = unit.at[rows] if hop == 0 else raw.at[way, 0, rows]
        to = (z + (1 if way == 0 else NZ - 1)) % NZ
        return pltpu.make_async_remote_copy(
            src_ref=src, dst_ref=raw.at[way, hop, rows],
            send_sem=raw_send.at[way, hop, piece], recv_sem=raw_recv.at[way, hop, piece],
            device_id=at(to, x, c, y), device_id_type=MESH,
        )

    pieces = ROWS // PIECE
    for piece in range(pieces):
        for way in range(2):
            raw_copy(way, 0, piece).start()

    def meta_copy(pos, sem):
        return pltpu.make_async_remote_copy(
            src_ref=meta.at[0], dst_ref=meta.at[pos],
            send_sem=meta_send.at[pos], recv_sem=meta_recv.at[sem],
            device_id=at(up(pos), x, c, y), device_id_type=MESH,
        )

    meta_copy(1, 0).start()
    meta_copy(2, 0).start()
    tell(0)
    learn(0)
    meta_copy(3, 0).start()
    meta_copy(4, 0).start()
    tell(1)
    learn(1)
    tell(2)

    def slots_of(code):
        return ((code >> 5) << 2) | (code & 3)

    def to_blocks(code, first, count, rows):
        line = iota((8 * count, ROWS), 0)
        pick = one_hot(slots_of(code) == ((first(line >> 3) << 2) | (line & 3)))
        twice = dot_nn(pick, rows)
        upper = (iota((8 * count, 128), 0) & 4) == 0
        thirds = [
            jnp.where(upper, twice[:, k : k + 128], twice[:, k + 128 : k + 256]).reshape(count, 8, 128)
            for k in range(0, D, 256)
        ]
        return jnp.concatenate(thirds, axis=1).astype(BF16)

    def is_here(j):
        return jnp.logical_and(j // 2 == x, handler_y(j) == y)

    def handler(zz, j):
        return at(zz, j // 2, c, handler_y(j))

    def block_copy(src, pos, zz, j, sem):
        return pltpu.make_async_remote_copy(
            src_ref=src, dst_ref=blocks.at[pos, xy], send_sem=sem, recv_sem=own_recv.at[pos],
            device_id=handler(zz, j), device_id_type=MESH,
        )

    def near_copy(pos, j):
        return block_copy(near_out.at[pos, j], pos, z, j, near_send.at[pos, j])

    def far_plane(way, g):
        return (z + (1 + g if way == 0 else NZ - 1 - g)) & (NZ - 1)

    def far_copy(way, g, j):
        return block_copy(far_out.at[way, g * 8 + j], 2 * g + 5 + way, far_plane(way, g), j, far_send.at[way])

    def opp_copy(way, j):
        zz = (z + (7 if way == 0 else NZ - 7)) & (NZ - 1)
        return block_copy(opp_out.at[way, j], 15, zz, way * 4 + j, opp_send.at[way])

    def send_near(pos, rows_ref):
        near_out[pos] = to_blocks(meta[pos], lambda j: z * 8 + j, 8, rows_ref[...])

        def send(j, _):
            @pl.when(is_here(j))
            def _():
                pltpu.make_async_copy(near_out.at[pos, j], blocks.at[pos, xy], own_recv.at[pos]).start()

            @pl.when(jnp.logical_not(is_here(j)))
            def _():
                near_copy(pos, j).start()
            return 0

        lax.fori_loop(0, 8, send, 0)

    for piece in range(pieces):
        for way in range(2):
            raw_copy(way, 0, piece).wait_recv()
            raw_copy(way, 1, piece).start()
        if piece == 0:
            learn(2)
            tell(3)
    near_meta = meta.at[pl.ds(1, 4)]
    pltpu.make_async_copy(near_meta, near_meta, meta_recv.at[0]).wait()
    learn(3)
    tell(4)

    def meta_start(pos, _):
        meta_copy(pos, 1).start()
        return 0

    lax.fori_loop(5, NZ, meta_start, 0)
    for way in range(2):
        zz = (z + (7 if way == 0 else NZ - 7)) & (NZ - 1)
        first = functools.partial(lambda base, j: base + j, zz * 8 + way * 4)
        opp_out[way] = to_blocks(meta[1 + way], first, 4, raw[way, 0])
    learn(4)
    for way in range(2):
        for j in range(4):
            opp_copy(way, j).start()
    send_near(0, unit)

    for way in range(2):
        for piece in range(pieces):
            raw_copy(way, 1, piece).wait_recv()

        def first(i, way=way):
            step = 1 + (i >> 3)
            return (((z + (step if way == 0 else NZ - step)) & (NZ - 1)) << 3) + (i & 7)

        far_out[way] = to_blocks(meta[3 + way], first, 40, raw[way, 1])
    for g in range(5):
        for way in range(2):
            def far_start(j, _, g=g, way=way):
                far_copy(way, g, j).start()
                return 0

            lax.fori_loop(0, 8, far_start, 0)
    send_near(1, raw.at[0, 0])
    send_near(2, raw.at[1, 0])
    send_near(3, raw.at[0, 1])
    send_near(4, raw.at[1, 1])

    i128 = iota((ROWS, ROWS), 0)
    lane = iota((ROWS, ROWS), 1)
    zq, j4 = (i128 >> 2) & 3, ((i128 >> 4) << 2) | (i128 & 3)

    def mine16():
        return pl.ds(pl.multiple_of(xy * 16, 16), 16)

    def ext_copy(j):
        return pltpu.make_async_remote_copy(
            src_ref=pext.at[j], dst_ref=ext_in.at[:, mine16()],
            send_sem=ext_send.at[j], recv_sem=ext_recv,
            device_id=at(z, j // 2, c, handler_y(j)), device_id_type=MESH,
        )

    far_meta = meta.at[pl.ds(5, NZ - 5)]
    pltpu.make_async_copy(far_meta, far_meta, meta_recv.at[1]).wait()
    for q in range(4):
        same = jnp.zeros((ROWS, EXT), F32)
        for k in range(4):
            code = meta[q * 4 + k]
            pick = one_hot((slots_of(code) == z * 32 + j4) & (zq == k))
            same += dot_nt(pick, one_hot((((code >> 2) & 7) == i128) | (i128 == 8)))
        right = jnp.where(lane < 8, PENALTY * same - PENALTY, jnp.where(lane == 8, -PENALTY * same, 0.0))
        pext[:, q] = right.astype(BF16).reshape(8, 16, EXT)

    def ext_start(j, _):
        @pl.when(is_here(j))
        def _():
            pltpu.make_async_copy(pext.at[j], ext_in.at[:, mine16()], ext_recv).start()

        @pl.when(jnp.logical_not(is_here(j)))
        def _():
            ext_copy(j).start()
        return 0

    lax.fori_loop(0, 8, ext_start, 0)

    def sib_copy(q, g):
        rows = pl.ds(pl.multiple_of(g * 64, 64), 64)
        return pltpu.make_async_remote_copy(
            src_ref=own.at[q, rows], dst_ref=sib.at[q, rows],
            send_sem=sib_send.at[q, g], recv_sem=sib_recv.at[q, g],
            device_id=at(z, x, 1 - c, y), device_id_type=MESH,
        )

    def terms(left_rows, right_rows):
        return jnp.exp2(dot_nt(left_rows, right_rows) * LOG2E10)

    def lane_sums(e):
        total = e[:, :128]
        for k in range(1, e.shape[1] // 128):
            total = total + e[:, k * 128 : k * 128 + 128]
        return total

    def permute_lanes():
        pltpu.make_async_copy(ext_in, ext_in, ext_recv).wait()
        row, col = iota((256, 256), 0), iota((256, 256), 1)
        order = one_hot(col == (((row >> 2) & 15) << 4) + ((row >> 6) << 2) + (row & 3))
        for k in range(4):
            own[k, :, D:] = dot_nn(order, ext_in[k]).astype(BF16)

    def take(q):
        row, col = iota((384, 384), 0), iota((384, 384), 1)
        line = ((row >> 2) & 15) * 24 + ((row >> 6) << 2) + (row & 3)
        unpack = one_hot(col == line)

        def one(k, _):
            pos = q * 4 + k
            pltpu.make_async_copy(blocks.at[pos], blocks.at[pos], own_recv.at[pos]).wait()
            lines = blocks[pos].astype(F32).reshape(384, 128).astype(BF16)
            parts = dot_nn(unpack, lines).astype(BF16)
            here = pl.ds(pl.multiple_of(k * 64, 64), 64)
            for i in range(6):
                own[q, here, i * 128 : i * 128 + 128] = parts[i * 64 : i * 64 + 64]
            sib_copy(q, k).start()
            return 0

        lax.fori_loop(0, 4, one, 0)

    def own_sums(q):
        old, new = q * 256, q * 256 + 256
        left[old:new, :D] = own[q, :, :D]
        is_cluster = iota((256, EXT), 1) < 9
        left[old:new, D:] = jnp.where(
            is_cluster, own[q, :, D:].astype(F32) * (1.0 / PENALTY) + 1.0, 0.0
        ).astype(BF16)
        e = terms(left[:new, :], own[q])
        sums = lane_sums(e)
        acc[old:new, :] = sums[old:]
        if q:
            acc[:old, :] = acc[:old, :] + sums[:old]
            colacc[q] = jnp.sum(e[:old].reshape(old // 8, 8, 256), axis=0)
        else:
            colacc[q] = jnp.zeros((8, 256), F32)

    def sib_sums(q):
        old, new = q * 256, q * 256 + 256

        def sib_wait(g, _):
            sib_copy(q, g).wait_recv()
            return 0

        lax.fori_loop(0, 4, sib_wait, 0)
        acc[:new, :] = acc[:new, :] + lane_sums(terms(left[:new, :], sib[q]))
        if q:
            e = terms(left[old:new, :], sib[:q].reshape(old, WIDE))
            acc[old:new, :] = acc[old:new, :] + lane_sums(e)

    @pl.when(handles)
    def _():
        permute_lanes()
        take(0)
        take(1)
        own_sums(0)
        own_sums(1)
        take(2)
        own_sums(2)
        sib_sums(0)
        sib_sums(1)
        take(3)
        sib_sums(2)
        own_sums(3)
        sib_sums(3)

    def tot_copy(i):
        return pltpu.make_async_remote_copy(
            src_ref=tot, dst_ref=back.at[my_owner],
            send_sem=tot_send.at[i], recv_sem=tot_recv,
            device_id=at(z, i // NY, c, i % NY), device_id_type=MESH,
        )

    @pl.when(handles)
    def _():
        for q in range(4):
            for h in range(2):
                part = acc[pl.ds(q * 256 + h * 128, 128), :].T
                total = jnp.sum(part, axis=0, keepdims=True) + jnp.sum(
                    colacc[q, :, h * 128 : h * 128 + 128], axis=0, keepdims=True
                )
                tot[q * 2 + h : q * 2 + h + 1, :] = total

        def send(i, _):
            @pl.when(i == xy)
            def _():
                pltpu.make_async_copy(tot, back.at[my_owner], tot_recv).start()

            @pl.when(i != xy)
            def _():
                tot_copy(i).start()
            return 0

        lax.fori_loop(0, NX * NY, send, 0)

    pltpu.make_async_copy(back, back, tot_recv).wait()
    for j in range(8):
        for k in range(8):
            ret[k, j : j + 1, :] = back[j, k : k + 1, :]

    def ret_copy(pos):
        return pltpu.make_async_remote_copy(
            src_ref=ret.at[pos // 2], dst_ref=wts.at[z],
            send_sem=ret_send.at[pos], recv_sem=ret_recv,
            device_id=at(down(pos), x, c, y), device_id_type=MESH,
        )

    def ret_start(pos, _):
        ret_copy(pos).start()
        return 0

    lax.fori_loop(1, NZ, ret_start, 0)
    wts[z] = ret[0]
    pltpu.make_async_copy(
        wts.at[pl.ds(0, NZ - 1)], wts.at[pl.ds(0, NZ - 1)], ret_recv
    ).wait()

    code = meta[0]
    table = wts[...].reshape(NZ * 8, 128).T
    lines = jnp.where((code >> 5) == iota((NZ * 8, ROWS), 0), 1.0, 0.0)
    picked = jnp.dot(table, lines, precision=lax.Precision.HIGHEST, preferred_element_type=F32)
    ahead = ((code >> 8) - z) & (NZ - 1)
    pos = jnp.where(ahead == 0, 0, jnp.where(ahead <= 8, 2 * ahead - 1, 2 * (NZ - ahead)))
    lane = (pos & 1) * 64 + xy * 4 + (code & 3)
    total = jnp.sum(jnp.where(iota((128, ROWS), 0) == lane, picked, 0.0), axis=0, keepdims=True)
    out_ref[...] = 0.1 * jnp.log(total)

    for way in range(2):
        for hop in range(2):
            for piece in range(pieces):
                raw_copy(way, hop, piece).wait_send()
        pltpu.make_async_copy(far_out.at[way], far_out.at[way], far_send.at[way]).wait()
        pltpu.make_async_copy(opp_out.at[way], opp_out.at[way], opp_send.at[way]).wait()

    def drain_z(pos, _):
        meta_copy(pos, 0).wait_send()
        ret_copy(pos).wait_send()
        return 0

    lax.fori_loop(1, NZ, drain_z, 0)

    def drain_plane(j, _):
        @pl.when(jnp.logical_not(is_here(j)))
        def _():
            ext_copy(j).wait_send()
            for pos in range(5):
                near_copy(pos, j).wait_send()
        return 0

    lax.fori_loop(0, 8, drain_plane, 0)

    @pl.when(handles)
    def _():
        def drain_sib(k, _):
            sib_copy(k >> 2, k & 3).wait_send()
            return 0

        lax.fori_loop(0, 16, drain_sib, 0)

        def drain_tot(i, _):
            @pl.when(i != xy)
            def _():
                tot_copy(i).wait_send()
            return 0

        lax.fori_loop(0, NX * NY, drain_tot, 0)


def per_device(embeddings, labels):
    dma = pltpu.SemaphoreType.DMA
    vmem = pltpu.VMEM
    weight = pl.pallas_call(
        kernel,
        out_shape=jax.ShapeDtypeStruct((1, ROWS), F32),
        in_specs=[pl.BlockSpec(memory_space=pltpu.HBM)] * 2,
        out_specs=pl.BlockSpec(memory_space=pltpu.VMEM),
        scratch_shapes=[
            vmem((ROWS, D), BF16),
            vmem((1, ROWS), jnp.int32),
            vmem((ROWS, D), BF16),
            vmem((2, 2, ROWS, D), BF16),
            vmem((NZ, 1, ROWS), jnp.int32),
            vmem((5, 8, 24, 128), BF16),
            vmem((2, 40, 24, 128), BF16),
            vmem((2, 4, 24, 128), BF16),
            vmem((NZ, 16, 24, 128), BF16),
            vmem((8, 4, 16, EXT), BF16),
            vmem((4, 256, EXT), BF16),
            vmem((4, 256, WIDE), BF16),
            vmem((4, 256, WIDE), BF16),
            vmem((1024, WIDE), BF16),
            vmem((1024, 128), F32),
            vmem((4, 8, 256), F32),
            vmem((8, 128), F32),
            vmem((8, 8, 128), F32),
            vmem((8, 8, 128), F32),
            vmem((NZ, 8, 128), F32),
            dma((2,)), pltpu.SemaphoreType.REGULAR((5,)),
            dma((2, 2, ROWS // PIECE)), dma((2, 2, ROWS // PIECE)),
            dma((5, 8)), dma((2,)), dma((2,)),
            dma((NZ,)), dma((2,)),
            dma((NZ,)),
            dma((8,)), dma,
            dma((4, 4)), dma((4, 4)),
            dma((NX * NY,)), dma,
            dma((NZ,)), dma,
        ],
        compiler_params=pltpu.CompilerParams(
            collective_id=0, has_side_effects=True, vmem_limit_bytes=64 * 1024 * 1024
        ),
        name="soft_dedup",
    )(embeddings, labels.reshape(1, ROWS))
    return weight.reshape(ROWS)


def solution(mesh):
    placed = (P(("shard", "split"), None), P(("shard", "split")))
    return jax.shard_map(
        per_device, mesh=mesh, in_specs=placed, out_specs=P(("shard", "split")), check_vma=False
    )
```

```python
import functools

import jax
import jax.numpy as jnp
from jax import lax
from jax.experimental import pallas as pl
from jax.experimental.pallas import tpu as pltpu
from jax.sharding import PartitionSpec as P

MESH = pl.DeviceIdType.MESH
F32 = jnp.float32
BF16 = jnp.bfloat16

D = 768
EXT = 128
WIDE = D + EXT
ROWS = 128
NZ, NX, NY = 16, 4, 4
PIECE = 64
PENALTY = 16.0
LOG2E10 = 14.426950408889634


def one_hot(cond):
    return jnp.where(cond, 1.0, 0.0).astype(BF16)


def dot_nn(a, b):
    return lax.dot_general(a, b, (((1,), (0,)), ((), ())), preferred_element_type=F32)


def dot_nt(a, b):
    return lax.dot_general(a, b, (((1,), (1,)), ((), ())), preferred_element_type=F32)


def seat(pos):
    return jnp.where(pos < 5, pos, 20 - pos) if not isinstance(pos, int) else pos if pos < 5 else 20 - pos


def iota(shape, dim):
    return lax.broadcasted_iota(jnp.int32, shape, dim)


def kernel(
    emb_hbm, lab_hbm, out_ref,
    emb, lab, unit, raw, meta, near_out, far_out, opp_out, blocks, pext, ext_in, own, sib, left, acc, colacc,
    tot, wts,
    in_sem, known, raw_send, raw_recv, near_send, far_send, opp_send, meta_send, meta_recv, own_recv,
    ext_send, ext_recv, sib_send, sib_recv, tot_send, tot_recv,
):
    p = lax.axis_index("shard")
    y = lax.axis_index("split")
    z = p >> 3
    x = (p >> 1) & 3
    c = p & 1
    xy = x * NY + y
    turn = (y - x + NY) & 3
    handles = (turn & 1) == 0
    my_owner = x * 2 + (turn >> 1)

    def at(zz, xx, cc, yy):
        return (zz * 8 + xx * 2 + cc, yy)

    def handler_y(j):
        return (2 * (j & 1) + (j >> 1)) & 3

    def up(pos):
        k = (pos + 1) >> 1
        return (z + jnp.where((pos & 1) == 1, k, NZ - k)) & (NZ - 1)

    def down(pos):
        k = (pos + 1) >> 1
        return (z + jnp.where((pos & 1) == 1, NZ - k, k)) & (NZ - 1)

    barrier = pltpu.get_barrier_semaphore()
    z_by = lambda k: at((z + k + NZ) & (NZ - 1), x, c, y)
    x_by = lambda k: at(z, (x + k) & 3, c, y)
    y_by = lambda k: at(z, x, c, (y + k) & 3)
    near = [z_by(1), z_by(-1), x_by(1), x_by(3), y_by(1), y_by(3)]
    for device in near + [at(z, x, 1 - c, y)]:
        pl.semaphore_signal(barrier, inc=1, device_id=device, device_id_type=MESH)
    load_emb = pltpu.make_async_copy(emb_hbm, emb, in_sem.at[0])
    load_lab = pltpu.make_async_copy(lab_hbm, lab, in_sem.at[1])
    load_lab.start()
    load_emb.start()

    rounds = [
        near,
        [z_by(2), z_by(-2)],
        [z_by(4), z_by(-4)],
        [y_by(1), y_by(2), y_by(3)],
        [x_by(1), x_by(2), x_by(3)],
    ]

    def tell(r):
        for device in rounds[r]:
            pl.semaphore_signal(known.at[r], inc=1, device_id=device, device_id_type=MESH)

    def learn(r):
        pl.semaphore_wait(known.at[r], len(rounds[r]))

    load_lab.wait()
    load_emb.wait()
    wide = emb[...].astype(F32)
    norm_sq = jnp.sum(wide * wide, axis=1, keepdims=True) + 1e-06
    unit[...] = (wide * lax.rsqrt(norm_sq)).astype(BF16)
    label = lab[...]
    owner = label >> 3
    owner_f = jnp.broadcast_to(owner.astype(F32), (ROWS, ROWS))
    earlier = (owner_f == owner_f.T) & (iota((ROWS, ROWS), 0) < iota((ROWS, ROWS), 1))
    rank = jnp.sum(jnp.where(earlier, 1.0, 0.0), axis=0, keepdims=True).astype(jnp.int32)
    meta[0] = label * 4 + rank

    pl.semaphore_wait(barrier, 7)

    def raw_copy(way, hop, piece):
        rows = pl.ds(piece * PIECE, PIECE)
        src = unit.at[rows] if hop == 0 else raw.at[way, 0, rows]
        to = (z + (1 if way == 0 else NZ - 1)) & (NZ - 1)
        return pltpu.make_async_remote_copy(
            src_ref=src, dst_ref=raw.at[way, hop, rows],
            send_sem=raw_send.at[way, hop, piece], recv_sem=raw_recv.at[way, hop, piece],
            device_id=at(to, x, c, y), device_id_type=MESH,
        )

    pieces = ROWS // PIECE
    for piece in range(pieces):
        for way in range(2):
            raw_copy(way, 0, piece).start()

    def meta_copy(pos, sem):
        return pltpu.make_async_remote_copy(
            src_ref=meta.at[0], dst_ref=meta.at[pos],
            send_sem=meta_send.at[pos], recv_sem=meta_recv.at[sem],
            device_id=at(up(pos), x, c, y), device_id_type=MESH,
        )

    meta_copy(1, 0).start()
    meta_copy(2, 0).start()
    tell(0)
    learn(0)
    meta_copy(3, 0).start()
    meta_copy(4, 0).start()
    tell(1)
    learn(1)
    tell(2)

    def slots_of(code):
        return ((code >> 5) << 2) | (code & 3)

    def to_blocks(code, first, count, rows):
        line = iota((8 * count, ROWS), 0)
        pick = one_hot(slots_of(code) == ((first(line >> 3) << 2) | (line & 3)))
        twice = dot_nn(pick, rows)
        upper = (iota((8 * count, 128), 0) & 4) == 0
        thirds = [
            jnp.where(upper, twice[:, k : k + 128], twice[:, k + 128 : k + 256]).reshape(count, 8, 128)
            for k in range(0, D, 256)
        ]
        return jnp.concatenate(thirds, axis=1).astype(BF16)

    def is_here(j):
        return jnp.logical_and((j >> 1) == x, handler_y(j) == y)

    def handler(zz, j):
        return at(zz, (j >> 1), c, handler_y(j))

    def block_copy(src, pos, zz, j, sem):
        return pltpu.make_async_remote_copy(
            src_ref=src, dst_ref=blocks.at[pos, xy], send_sem=sem, recv_sem=own_recv.at[pos],
            device_id=handler(zz, j), device_id_type=MESH,
        )

    def near_copy(pos, j):
        return block_copy(near_out.at[pos, j], pos, z, j, near_send.at[pos, j])

    def far_plane(way, g):
        return (z + (1 + g if way == 0 else NZ - 1 - g)) & (NZ - 1)

    def far_copy(way, g, j):
        return block_copy(far_out.at[way, g * 8 + j], 2 * g + 5 + way, far_plane(way, g), j, far_send.at[way])

    def opp_copy(way, j):
        zz = (z + (7 if way == 0 else NZ - 7)) & (NZ - 1)
        return block_copy(opp_out.at[way, j], 15, zz, way * 4 + j, opp_send.at[way])

    def send_near(pos, rows_ref):
        near_out[pos] = to_blocks(meta[pos], lambda j: z * 8 + j, 8, rows_ref[...])

        def send(j, _):
            @pl.when(is_here(j))
            def _():
                pltpu.make_async_copy(near_out.at[pos, j], blocks.at[pos, xy], own_recv.at[pos]).start()

            @pl.when(jnp.logical_not(is_here(j)))
            def _():
                near_copy(pos, j).start()
            return 0

        lax.fori_loop(0, 8, send, 0)

    for piece in range(pieces):
        for way in range(2):
            raw_copy(way, 0, piece).wait_recv()
            raw_copy(way, 1, piece).start()
        if piece == 0:
            learn(2)
            tell(3)
    near_meta = meta.at[pl.ds(1, 4)]
    pltpu.make_async_copy(near_meta, near_meta, meta_recv.at[0]).wait()
    learn(3)
    tell(4)

    def meta_start(pos, _):
        meta_copy(pos, 1).start()
        return 0

    lax.fori_loop(5, NZ, meta_start, 0)
    for way in range(2):
        zz = (z + (7 if way == 0 else NZ - 7)) & (NZ - 1)
        first = functools.partial(lambda base, j: base + j, zz * 8 + way * 4)
        opp_out[way] = to_blocks(meta[1 + way], first, 4, raw[way, 0])
    learn(4)
    for way in range(2):
        for j in range(4):
            opp_copy(way, j).start()
    send_near(0, unit)

    for way in range(2):
        for piece in range(pieces):
            raw_copy(way, 1, piece).wait_recv()

        def first(i, way=way):
            step = 1 + (i >> 3)
            return (((z + (step if way == 0 else NZ - step)) & (NZ - 1)) << 3) + (i & 7)

        far_out[way] = to_blocks(meta[3 + way], first, 40, raw[way, 1])

    def send_far(g):
        for way in range(2):
            def far_start(j, _, way=way):
                far_copy(way, g, j).start()
                return 0

            lax.fori_loop(0, 8, far_start, 0)

    for g in (4, 3, 2, 1, 0):
        send_far(g)
    send_near(1, raw.at[0, 0])
    send_near(2, raw.at[1, 0])
    send_near(3, raw.at[0, 1])
    send_near(4, raw.at[1, 1])

    i128 = iota((ROWS, ROWS), 0)
    lane = iota((ROWS, ROWS), 1)
    zq, j4 = (i128 >> 2) & 3, ((i128 >> 4) << 2) | (i128 & 3)

    def mine16():
        return pl.ds(pl.multiple_of(xy * 16, 16), 16)

    def ext_copy(j):
        return pltpu.make_async_remote_copy(
            src_ref=pext.at[j], dst_ref=ext_in.at[:, mine16()],
            send_sem=ext_send.at[j], recv_sem=ext_recv,
            device_id=at(z, (j >> 1), c, handler_y(j)), device_id_type=MESH,
        )

    far_meta = meta.at[pl.ds(5, NZ - 5)]
    pltpu.make_async_copy(far_meta, far_meta, meta_recv.at[1]).wait()
    for q in range(4):
        same = jnp.zeros((ROWS, EXT), F32)
        for k in range(4):
            code = meta[seat(q * 4 + k)]
            pick = one_hot((slots_of(code) == z * 32 + j4) & (zq == k))
            same += dot_nt(pick, one_hot((((code >> 2) & 7) == i128) | (i128 == 8)))
        right = jnp.where(lane < 8, PENALTY * same - PENALTY, jnp.where(lane == 8, -PENALTY * same, 0.0))
        pext[:, q] = right.astype(BF16).reshape(8, 16, EXT)

    def ext_start(j, _):
        @pl.when(is_here(j))
        def _():
            pltpu.make_async_copy(pext.at[j], ext_in.at[:, mine16()], ext_recv).start()

        @pl.when(jnp.logical_not(is_here(j)))
        def _():
            ext_copy(j).start()
        return 0

    lax.fori_loop(0, 8, ext_start, 0)

    def sib_copy(q, g):
        rows = pl.ds(pl.multiple_of(g * 64, 64), 64)
        return pltpu.make_async_remote_copy(
            src_ref=own.at[q, rows], dst_ref=sib.at[q, rows],
            send_sem=sib_send.at[q, g], recv_sem=sib_recv.at[q, g],
            device_id=at(z, x, 1 - c, y), device_id_type=MESH,
        )

    def terms(left_rows, right_rows):
        return jnp.exp2(dot_nt(left_rows, right_rows) * LOG2E10)

    def lane_sums(e):
        total = e[:, :128]
        for k in range(1, e.shape[1] // 128):
            total = total + e[:, k * 128 : k * 128 + 128]
        return total

    def permute_lanes():
        pltpu.make_async_copy(ext_in, ext_in, ext_recv).wait()
        row, col = iota((256, 256), 0), iota((256, 256), 1)
        order = one_hot(col == (((row >> 2) & 15) << 4) + ((row >> 6) << 2) + (row & 3))
        for k in range(4):
            own[k, :, D:] = dot_nn(order, ext_in[k]).astype(BF16)

    def take(q):
        row, col = iota((384, 384), 0), iota((384, 384), 1)
        line = ((row >> 2) & 15) * 24 + ((row >> 6) << 2) + (row & 3)
        unpack = one_hot(col == line)

        def one(k, _):
            pos = seat(q * 4 + k)
            pltpu.make_async_copy(blocks.at[pos], blocks.at[pos], own_recv.at[pos]).wait()
            lines = blocks[pos].astype(F32).reshape(384, 128).astype(BF16)
            parts = dot_nn(unpack, lines).astype(BF16)
            here = pl.ds(pl.multiple_of(k * 64, 64), 64)
            for i in range(6):
                own[q, here, i * 128 : i * 128 + 128] = parts[i * 64 : i * 64 + 64]
            sib_copy(q, k).start()
            return 0

        lax.fori_loop(0, 4, one, 0)

    def own_sums(q):
        old, new = q * 256, q * 256 + 256
        left[old:new, :D] = own[q, :, :D]
        is_cluster = iota((256, EXT), 1) < 9
        left[old:new, D:] = jnp.where(
            is_cluster, own[q, :, D:].astype(F32) * (1.0 / PENALTY) + 1.0, 0.0
        ).astype(BF16)
        e = terms(left[:new, :], own[q])
        sums = lane_sums(e)
        acc[old:new, :] = sums[old:]
        if q:
            acc[:old, :] = acc[:old, :] + sums[:old]
            colacc[q] = jnp.sum(e[:old].reshape(old // 8, 8, 256), axis=0)
        else:
            colacc[q] = jnp.zeros((8, 256), F32)

    def sib_sums(q):
        old, new = q * 256, q * 256 + 256

        def sib_wait(g, _):
            sib_copy(q, g).wait_recv()
            return 0

        lax.fori_loop(0, 4, sib_wait, 0)
        acc[:new, :] = acc[:new, :] + lane_sums(terms(left[:new, :], sib[q]))
        if q:
            e = terms(left[old:new, :], sib[:q].reshape(old, WIDE))
            acc[old:new, :] = acc[old:new, :] + lane_sums(e)

    @pl.when(handles)
    def _():
        permute_lanes()
        take(0)
        take(1)
        own_sums(0)
        own_sums(1)
        sib_sums(0)
        take(2)
        own_sums(2)
        sib_sums(1)
        take(3)
        sib_sums(2)
        own_sums(3)
        sib_sums(3)

    def tot_copy(i):
        pos, to = 15 - (i >> 4), i & 15
        return pltpu.make_async_remote_copy(
            src_ref=tot.at[seat(pos) >> 1], dst_ref=wts.at[z * 8 + my_owner],
            send_sem=tot_send, recv_sem=tot_recv,
            device_id=at(down(pos), to >> 2, c, to & 3), device_id_type=MESH,
        )

    @pl.when(handles)
    def _():
        for q in range(4):
            for h in range(2):
                part = acc[pl.ds(q * 256 + h * 128, 128), :].T
                total = jnp.sum(part, axis=0, keepdims=True) + jnp.sum(
                    colacc[q, :, h * 128 : h * 128 + 128], axis=0, keepdims=True
                )
                tot[q * 2 + h] = total

        def send(i, _):
            tot_copy(i).start()
            return 0

        def send_here(i, _):
            @pl.when(i - 240 != xy)
            def _():
                tot_copy(i).start()
            return 0

        lax.fori_loop(0, 240, send, 0)
        pltpu.make_async_copy(tot.at[0], wts.at[z * 8 + my_owner], tot_recv).start()
        lax.fori_loop(240, 256, send_here, 0)

    arrived = wts.at[pl.ds(0, NZ * 8)]
    pltpu.make_async_copy(arrived, arrived, tot_recv).wait()

    code = meta[0]
    table = wts[: NZ * 8].reshape(NZ * 8, 128).T
    lines = jnp.where((code >> 5) == iota((NZ * 8, ROWS), 0), 1.0, 0.0)
    picked = jnp.dot(table, lines, precision=lax.Precision.HIGHEST, preferred_element_type=F32)
    ahead = ((code >> 8) - z) & (NZ - 1)
    pos = jnp.where(ahead == 0, 0, jnp.where(ahead <= 8, 2 * ahead - 1, 2 * (NZ - ahead)))
    lane = (seat(pos) & 1) * 64 + xy * 4 + (code & 3)
    total = jnp.sum(jnp.where(iota((128, ROWS), 0) == lane, picked, 0.0), axis=0, keepdims=True)
    out_ref[...] = 0.1 * jnp.log(total)

    for way in range(2):
        for hop in range(2):
            for piece in range(pieces):
                raw_copy(way, hop, piece).wait_send()
        pltpu.make_async_copy(far_out.at[way], far_out.at[way], far_send.at[way]).wait()
        pltpu.make_async_copy(opp_out.at[way], opp_out.at[way], opp_send.at[way]).wait()

    def drain_z(pos, _):
        meta_copy(pos, 0).wait_send()
        return 0

    lax.fori_loop(1, NZ, drain_z, 0)

    def drain_plane(j, _):
        @pl.when(jnp.logical_not(is_here(j)))
        def _():
            ext_copy(j).wait_send()
            for pos in range(5):
                near_copy(pos, j).wait_send()
        return 0

    lax.fori_loop(0, 8, drain_plane, 0)

    @pl.when(handles)
    def _():
        def drain_sib(k, _):
            sib_copy(k >> 2, k & 3).wait_send()
            return 0

        lax.fori_loop(0, 16, drain_sib, 0)

        sent = wts.at[pl.ds(0, 255)]
        pltpu.make_async_copy(sent, sent, tot_send).wait()


def per_device(embeddings, labels):
    dma = pltpu.SemaphoreType.DMA
    vmem = pltpu.VMEM
    weight = pl.pallas_call(
        kernel,
        out_shape=jax.ShapeDtypeStruct((1, ROWS), F32),
        in_specs=[pl.BlockSpec(memory_space=pltpu.HBM)] * 2,
        out_specs=pl.BlockSpec(memory_space=pltpu.VMEM),
        scratch_shapes=[
            vmem((ROWS, D), BF16),
            vmem((1, ROWS), jnp.int32),
            vmem((ROWS, D), BF16),
            vmem((2, 2, ROWS, D), BF16),
            vmem((NZ, 1, ROWS), jnp.int32),
            vmem((5, 8, 24, 128), BF16),
            vmem((2, 40, 24, 128), BF16),
            vmem((2, 4, 24, 128), BF16),
            vmem((NZ, 16, 24, 128), BF16),
            vmem((8, 4, 16, EXT), BF16),
            vmem((4, 256, EXT), BF16),
            vmem((4, 256, WIDE), BF16),
            vmem((4, 256, WIDE), BF16),
            vmem((1024, WIDE), BF16),
            vmem((1024, 128), F32),
            vmem((4, 8, 256), F32),
            vmem((8, 1, 128), F32),
            vmem((2 * NZ * 8, 1, 128), F32),
            dma((2,)), pltpu.SemaphoreType.REGULAR((5,)),
            dma((2, 2, ROWS // PIECE)), dma((2, 2, ROWS // PIECE)),
            dma((5, 8)), dma((2,)), dma((2,)),
            dma((NZ,)), dma((2,)),
            dma((NZ,)),
            dma((8,)), dma,
            dma((4, 4)), dma((4, 4)),
            dma, dma,
        ],
        compiler_params=pltpu.CompilerParams(
            collective_id=0, has_side_effects=True, vmem_limit_bytes=64 * 1024 * 1024
        ),
        name="soft_dedup",
    )(embeddings, labels.reshape(1, ROWS))
    return weight.reshape(ROWS)


def solution(mesh):
    placed = (P(("shard", "split"), None), P(("shard", "split")))
    return jax.shard_map(
        per_device, mesh=mesh, in_specs=placed, out_specs=P(("shard", "split")), check_vma=False
    )
```

```python
import functools

import jax
import jax.numpy as jnp
from jax import lax
from jax.experimental import pallas as pl
from jax.experimental.pallas import tpu as pltpu
from jax.sharding import PartitionSpec as P

MESH = pl.DeviceIdType.MESH
F32 = jnp.float32
BF16 = jnp.bfloat16

D = 768
EXT = 128
WIDE = D + EXT
ROWS = 128
NZ, NX, NY = 16, 4, 4
PIECE = 64
PENALTY = 16.0
LOG2E10 = 14.426950408889634


def one_hot(cond):
    return jnp.where(cond, 1.0, 0.0).astype(BF16)


def dot_nn(a, b):
    return lax.dot_general(a, b, (((1,), (0,)), ((), ())), preferred_element_type=F32)


def dot_nt(a, b):
    return lax.dot_general(a, b, (((1,), (1,)), ((), ())), preferred_element_type=F32)


def seat(pos):
    return jnp.where(pos < 5, pos, 20 - pos) if not isinstance(pos, int) else pos if pos < 5 else 20 - pos


def iota(shape, dim):
    return lax.broadcasted_iota(jnp.int32, shape, dim)


def kernel(
    emb_hbm, lab_hbm, out_ref,
    emb, lab, unit, raw, meta, near_out, far_out, opp_out, blocks, pext, ext_in, own, sib, left, acc, colacc,
    tot, wts,
    in_sem, known, raw_send, raw_recv, near_send, far_send, opp_send, meta_send, meta_recv, own_recv,
    ext_send, ext_recv, sib_send, sib_recv, tot_send, tot_recv,
):
    p = lax.axis_index("shard")
    y = lax.axis_index("split")
    z = p >> 3
    x = (p >> 1) & 3
    c = p & 1
    xy = x * NY + y
    turn = (y - x + NY) & 3
    handles = (turn & 1) == 0
    my_owner = x * 2 + (turn >> 1)

    def at(zz, xx, cc, yy):
        return (zz * 8 + xx * 2 + cc, yy)

    def handler_y(j):
        return (2 * (j & 1) + (j >> 1)) & 3

    def up(pos):
        k = (pos + 1) >> 1
        return (z + jnp.where((pos & 1) == 1, k, NZ - k)) & (NZ - 1)

    def down(pos):
        k = (pos + 1) >> 1
        return (z + jnp.where((pos & 1) == 1, NZ - k, k)) & (NZ - 1)

    barrier = pltpu.get_barrier_semaphore()
    z_by = lambda k: at((z + k + NZ) & (NZ - 1), x, c, y)
    x_by = lambda k: at(z, (x + k) & 3, c, y)
    y_by = lambda k: at(z, x, c, (y + k) & 3)
    near = [z_by(1), z_by(-1), x_by(1), x_by(3), y_by(1), y_by(3)]
    for device in near + [at(z, x, 1 - c, y)]:
        pl.semaphore_signal(barrier, inc=1, device_id=device, device_id_type=MESH)
    load_emb = pltpu.make_async_copy(emb_hbm, emb, in_sem.at[0])
    load_lab = pltpu.make_async_copy(lab_hbm, lab, in_sem.at[1])
    load_lab.start()
    load_emb.start()

    rounds = [
        near,
        [z_by(2), z_by(-2)],
        [z_by(4), z_by(-4)],
        [y_by(1), y_by(2), y_by(3)],
        [x_by(1), x_by(2), x_by(3)],
    ]

    def tell(r):
        for device in rounds[r]:
            pl.semaphore_signal(known.at[r], inc=1, device_id=device, device_id_type=MESH)

    def learn(r):
        pl.semaphore_wait(known.at[r], len(rounds[r]))

    load_lab.wait()
    load_emb.wait()
    wide = emb[...].astype(F32)
    norm_sq = jnp.sum(wide * wide, axis=1, keepdims=True) + 1e-06
    unit[...] = (wide * lax.rsqrt(norm_sq)).astype(BF16)
    label = lab[...]
    owner = label >> 3
    owner_f = jnp.broadcast_to(owner.astype(F32), (ROWS, ROWS))
    earlier = (owner_f == owner_f.T) & (iota((ROWS, ROWS), 0) < iota((ROWS, ROWS), 1))
    rank = jnp.sum(jnp.where(earlier, 1.0, 0.0), axis=0, keepdims=True).astype(jnp.int32)
    meta[0] = label * 4 + rank

    pl.semaphore_wait(barrier, 7)

    def raw_copy(way, hop, piece):
        rows = pl.ds(piece * PIECE, PIECE)
        src = unit.at[rows] if hop == 0 else raw.at[way, 0, rows]
        to = (z + (1 if way == 0 else NZ - 1)) & (NZ - 1)
        return pltpu.make_async_remote_copy(
            src_ref=src, dst_ref=raw.at[way, hop, rows],
            send_sem=raw_send.at[way, hop, piece], recv_sem=raw_recv.at[way, hop, piece],
            device_id=at(to, x, c, y), device_id_type=MESH,
        )

    pieces = ROWS // PIECE
    for piece in range(pieces):
        for way in range(2):
            raw_copy(way, 0, piece).start()

    def meta_copy(pos, sem):
        return pltpu.make_async_remote_copy(
            src_ref=meta.at[0], dst_ref=meta.at[pos],
            send_sem=meta_send.at[pos], recv_sem=meta_recv.at[sem],
            device_id=at(up(pos), x, c, y), device_id_type=MESH,
        )

    meta_copy(1, 0).start()
    meta_copy(2, 0).start()
    tell(0)
    learn(0)
    meta_copy(3, 0).start()
    meta_copy(4, 0).start()
    tell(1)
    learn(1)
    tell(2)

    def slots_of(code):
        return ((code >> 5) << 2) | (code & 3)

    def to_blocks(code, first, count, rows):
        line = iota((8 * count, ROWS), 0)
        pick = one_hot(slots_of(code) == ((first(line >> 3) << 2) | (line & 3)))
        twice = dot_nn(pick, rows)
        upper = (iota((8 * count, 128), 0) & 4) == 0
        thirds = [
            jnp.where(upper, twice[:, k : k + 128], twice[:, k + 128 : k + 256]).reshape(count, 8, 128)
            for k in range(0, D, 256)
        ]
        return jnp.concatenate(thirds, axis=1).astype(BF16)

    def is_here(j):
        return jnp.logical_and((j >> 1) == x, handler_y(j) == y)

    def handler(zz, j):
        return at(zz, (j >> 1), c, handler_y(j))

    def block_copy(src, pos, zz, j, sem):
        return pltpu.make_async_remote_copy(
            src_ref=src, dst_ref=blocks.at[pos, xy], send_sem=sem, recv_sem=own_recv.at[pos],
            device_id=handler(zz, j), device_id_type=MESH,
        )

    def near_copy(pos, j):
        return block_copy(near_out.at[pos, j], pos, z, j, near_send.at[pos, j])

    def far_plane(way, g):
        return (z + (1 + g if way == 0 else NZ - 1 - g)) & (NZ - 1)

    def far_copy(way, g, j):
        return block_copy(far_out.at[way, g * 8 + j], 2 * g + 5 + way, far_plane(way, g), j, far_send.at[way])

    def opp_copy(way, j):
        zz = (z + (7 if way == 0 else NZ - 7)) & (NZ - 1)
        return block_copy(opp_out.at[way, j], 15, zz, way * 4 + j, opp_send.at[way])

    def send_near(pos, rows_ref):
        near_out[pos] = to_blocks(meta[pos], lambda j: z * 8 + j, 8, rows_ref[...])

        def send(j, _):
            @pl.when(is_here(j))
            def _():
                pltpu.make_async_copy(near_out.at[pos, j], blocks.at[pos, xy], own_recv.at[pos]).start()

            @pl.when(jnp.logical_not(is_here(j)))
            def _():
                near_copy(pos, j).start()
            return 0

        lax.fori_loop(0, 8, send, 0)

    for piece in range(pieces):
        for way in range(2):
            raw_copy(way, 0, piece).wait_recv()
            raw_copy(way, 1, piece).start()
        if piece == 0:
            learn(2)
            tell(3)
    near_meta = meta.at[pl.ds(1, 4)]
    pltpu.make_async_copy(near_meta, near_meta, meta_recv.at[0]).wait()
    learn(3)
    tell(4)

    def meta_start(pos, _):
        meta_copy(pos, 1).start()
        return 0

    lax.fori_loop(5, NZ, meta_start, 0)
    for way in range(2):
        zz = (z + (7 if way == 0 else NZ - 7)) & (NZ - 1)
        first = functools.partial(lambda base, j: base + j, zz * 8 + way * 4)
        opp_out[way] = to_blocks(meta[1 + way], first, 4, raw[way, 0])
    learn(4)
    for way in range(2):
        for j in range(4):
            opp_copy(way, j).start()
    send_near(0, unit)
    send_near(1, raw.at[0, 0])
    send_near(2, raw.at[1, 0])

    for way in range(2):
        for piece in range(pieces):
            raw_copy(way, 1, piece).wait_recv()

        def first(i, way=way):
            step = 1 + (i >> 3)
            return (((z + (step if way == 0 else NZ - step)) & (NZ - 1)) << 3) + (i & 7)

        far_out[way] = to_blocks(meta[3 + way], first, 40, raw[way, 1])

    def send_far(g):
        for way in range(2):
            def far_start(j, _, way=way):
                far_copy(way, g, j).start()
                return 0

            lax.fori_loop(0, 8, far_start, 0, unroll=True)

    for g in (4, 3, 2, 1, 0):
        send_far(g)
    send_near(3, raw.at[0, 1])
    send_near(4, raw.at[1, 1])

    i128 = iota((ROWS, ROWS), 0)
    lane = iota((ROWS, ROWS), 1)
    zq, j4 = (i128 >> 2) & 3, ((i128 >> 4) << 2) | (i128 & 3)

    def mine16():
        return pl.ds(pl.multiple_of(xy * 16, 16), 16)

    def ext_copy(j):
        return pltpu.make_async_remote_copy(
            src_ref=pext.at[j], dst_ref=ext_in.at[:, mine16()],
            send_sem=ext_send.at[j], recv_sem=ext_recv,
            device_id=at(z, (j >> 1), c, handler_y(j)), device_id_type=MESH,
        )

    far_meta = meta.at[pl.ds(5, NZ - 5)]
    pltpu.make_async_copy(far_meta, far_meta, meta_recv.at[1]).wait()
    for q in range(4):
        same = jnp.zeros((ROWS, EXT), F32)
        for k in range(4):
            code = meta[seat(q * 4 + k)]
            pick = one_hot((slots_of(code) == z * 32 + j4) & (zq == k))
            same += dot_nt(pick, one_hot((((code >> 2) & 7) == i128) | (i128 == 8)))
        right = jnp.where(lane < 8, PENALTY * same - PENALTY, jnp.where(lane == 8, -PENALTY * same, 0.0))
        pext[:, q] = right.astype(BF16).reshape(8, 16, EXT)

    def ext_start(j, _):
        @pl.when(is_here(j))
        def _():
            pltpu.make_async_copy(pext.at[j], ext_in.at[:, mine16()], ext_recv).start()

        @pl.when(jnp.logical_not(is_here(j)))
        def _():
            ext_copy(j).start()
        return 0

    lax.fori_loop(0, 8, ext_start, 0)

    def sib_copy(q, g):
        rows = pl.ds(pl.multiple_of(g * 64, 64), 64)
        return pltpu.make_async_remote_copy(
            src_ref=own.at[q, rows], dst_ref=sib.at[q, rows],
            send_sem=sib_send.at[q, g], recv_sem=sib_recv.at[q, g],
            device_id=at(z, x, 1 - c, y), device_id_type=MESH,
        )

    def terms(left_rows, right_rows):
        return jnp.exp2(dot_nt(left_rows, right_rows) * LOG2E10)

    def lane_sums(e):
        total = e[:, :128]
        for k in range(1, e.shape[1] // 128):
            total = total + e[:, k * 128 : k * 128 + 128]
        return total

    def permute_lanes():
        pltpu.make_async_copy(ext_in, ext_in, ext_recv).wait()
        row, col = iota((256, 256), 0), iota((256, 256), 1)
        order = one_hot(col == (((row >> 2) & 15) << 4) + ((row >> 6) << 2) + (row & 3))
        for k in range(4):
            own[k, :, D:] = dot_nn(order, ext_in[k]).astype(BF16)

    def take(q):
        row, col = iota((384, 384), 0), iota((384, 384), 1)
        line = ((row >> 2) & 15) * 24 + ((row >> 6) << 2) + (row & 3)
        unpack = one_hot(col == line)

        def one(k, _):
            pos = seat(q * 4 + k)
            pltpu.make_async_copy(blocks.at[pos], blocks.at[pos], own_recv.at[pos]).wait()
            lines = blocks[pos].astype(F32).reshape(384, 128).astype(BF16)
            parts = dot_nn(unpack, lines).astype(BF16)
            here = pl.ds(pl.multiple_of(k * 64, 64), 64)
            for i in range(6):
                own[q, here, i * 128 : i * 128 + 128] = parts[i * 64 : i * 64 + 64]
            sib_copy(q, k).start()
            return 0

        lax.fori_loop(0, 4, one, 0)

    def own_sums(q):
        old, new = q * 256, q * 256 + 256
        left[old:new, :D] = own[q, :, :D]
        is_cluster = iota((256, EXT), 1) < 9
        left[old:new, D:] = jnp.where(
            is_cluster, own[q, :, D:].astype(F32) * (1.0 / PENALTY) + 1.0, 0.0
        ).astype(BF16)
        e = terms(left[:new, :], own[q])
        sums = lane_sums(e)
        acc[old:new, :] = sums[old:]
        if q:
            acc[:old, :] = acc[:old, :] + sums[:old]
            colacc[q] = jnp.sum(e[:old].reshape(old // 8, 8, 256), axis=0)
        else:
            colacc[q] = jnp.zeros((8, 256), F32)

    def sib_sums(q):
        old, new = q * 256, q * 256 + 256

        def sib_wait(g, _):
            sib_copy(q, g).wait_recv()
            return 0

        lax.fori_loop(0, 4, sib_wait, 0)
        acc[:new, :] = acc[:new, :] + lane_sums(terms(left[:new, :], sib[q]))
        if q:
            e = terms(left[old:new, :], sib[:q].reshape(old, WIDE))
            acc[old:new, :] = acc[old:new, :] + lane_sums(e)

    @pl.when(handles)
    def _():
        permute_lanes()
        take(0)
        take(1)
        own_sums(0)
        own_sums(1)
        sib_sums(0)
        take(2)
        own_sums(2)
        sib_sums(1)
        take(3)
        sib_sums(2)
        own_sums(3)
        sib_sums(3)

    def tot_copy(i):
        pos, to = 15 - (i >> 4), i & 15
        return pltpu.make_async_remote_copy(
            src_ref=tot.at[seat(pos) >> 1], dst_ref=wts.at[z * 8 + my_owner],
            send_sem=tot_send, recv_sem=tot_recv,
            device_id=at(down(pos), to >> 2, c, to & 3), device_id_type=MESH,
        )

    @pl.when(handles)
    def _():
        for q in range(4):
            for h in range(2):
                part = acc[pl.ds(q * 256 + h * 128, 128), :].T
                total = jnp.sum(part, axis=0, keepdims=True) + jnp.sum(
                    colacc[q, :, h * 128 : h * 128 + 128], axis=0, keepdims=True
                )
                tot[q * 2 + h] = total

        def send(i, _):
            tot_copy(i).start()
            return 0

        def send_here(i, _):
            @pl.when(i - 240 != xy)
            def _():
                tot_copy(i).start()
            return 0

        lax.fori_loop(0, 240, send, 0, unroll=8)
        pltpu.make_async_copy(tot.at[0], wts.at[z * 8 + my_owner], tot_recv).start()
        lax.fori_loop(240, 256, send_here, 0)

    arrived = wts.at[pl.ds(0, NZ * 8)]
    pltpu.make_async_copy(arrived, arrived, tot_recv).wait()

    code = meta[0]
    table = wts[: NZ * 8].reshape(NZ * 8, 128).T
    lines = jnp.where((code >> 5) == iota((NZ * 8, ROWS), 0), 1.0, 0.0)
    picked = jnp.dot(table, lines, precision=lax.Precision.HIGHEST, preferred_element_type=F32)
    ahead = ((code >> 8) - z) & (NZ - 1)
    pos = jnp.where(ahead == 0, 0, jnp.where(ahead <= 8, 2 * ahead - 1, 2 * (NZ - ahead)))
    lane = (seat(pos) & 1) * 64 + xy * 4 + (code & 3)
    total = jnp.sum(jnp.where(iota((128, ROWS), 0) == lane, picked, 0.0), axis=0, keepdims=True)
    out_ref[...] = 0.1 * jnp.log(total)

    for way in range(2):
        for hop in range(2):
            for piece in range(pieces):
                raw_copy(way, hop, piece).wait_send()
        pltpu.make_async_copy(far_out.at[way], far_out.at[way], far_send.at[way]).wait()
        pltpu.make_async_copy(opp_out.at[way], opp_out.at[way], opp_send.at[way]).wait()

    def drain_z(pos, _):
        meta_copy(pos, 0).wait_send()
        return 0

    lax.fori_loop(1, NZ, drain_z, 0)

    def drain_plane(j, _):
        @pl.when(jnp.logical_not(is_here(j)))
        def _():
            ext_copy(j).wait_send()
            for pos in range(5):
                near_copy(pos, j).wait_send()
        return 0

    lax.fori_loop(0, 8, drain_plane, 0)

    @pl.when(handles)
    def _():
        def drain_sib(k, _):
            sib_copy(k >> 2, k & 3).wait_send()
            return 0

        lax.fori_loop(0, 16, drain_sib, 0)

        sent = wts.at[pl.ds(0, 255)]
        pltpu.make_async_copy(sent, sent, tot_send).wait()


def per_device(embeddings, labels):
    dma = pltpu.SemaphoreType.DMA
    vmem = pltpu.VMEM
    weight = pl.pallas_call(
        kernel,
        out_shape=jax.ShapeDtypeStruct((1, ROWS), F32),
        in_specs=[pl.BlockSpec(memory_space=pltpu.HBM)] * 2,
        out_specs=pl.BlockSpec(memory_space=pltpu.VMEM),
        scratch_shapes=[
            vmem((ROWS, D), BF16),
            vmem((1, ROWS), jnp.int32),
            vmem((ROWS, D), BF16),
            vmem((2, 2, ROWS, D), BF16),
            vmem((NZ, 1, ROWS), jnp.int32),
            vmem((5, 8, 24, 128), BF16),
            vmem((2, 40, 24, 128), BF16),
            vmem((2, 4, 24, 128), BF16),
            vmem((NZ, 16, 24, 128), BF16),
            vmem((8, 4, 16, EXT), BF16),
            vmem((4, 256, EXT), BF16),
            vmem((4, 256, WIDE), BF16),
            vmem((4, 256, WIDE), BF16),
            vmem((1024, WIDE), BF16),
            vmem((1024, 128), F32),
            vmem((4, 8, 256), F32),
            vmem((8, 1, 128), F32),
            vmem((2 * NZ * 8, 1, 128), F32),
            dma((2,)), pltpu.SemaphoreType.REGULAR((5,)),
            dma((2, 2, ROWS // PIECE)), dma((2, 2, ROWS // PIECE)),
            dma((5, 8)), dma((2,)), dma((2,)),
            dma((NZ,)), dma((2,)),
            dma((NZ,)),
            dma((8,)), dma,
            dma((4, 4)), dma((4, 4)),
            dma, dma,
        ],
        compiler_params=pltpu.CompilerParams(
            collective_id=0, has_side_effects=True, vmem_limit_bytes=64 * 1024 * 1024
        ),
        name="soft_dedup",
    )(embeddings, labels.reshape(1, ROWS))
    return weight.reshape(ROWS)


def solution(mesh):
    placed = (P(("shard", "split"), None), P(("shard", "split")))
    return jax.shard_map(
        per_device, mesh=mesh, in_specs=placed, out_specs=P(("shard", "split")), check_vma=False
    )
```

```python
import functools

import jax
import jax.numpy as jnp
from jax import lax
from jax.experimental import pallas as pl
from jax.experimental.pallas import tpu as pltpu
from jax.sharding import PartitionSpec as P

MESH = pl.DeviceIdType.MESH
F32 = jnp.float32
BF16 = jnp.bfloat16

D = 768
EXT = 128
WIDE = D + EXT
ROWS = 128
NZ, NX, NY = 16, 4, 4
PIECE = 64
PENALTY = 16.0
LOG2E10 = 14.426950408889634


def one_hot(cond):
    return jnp.where(cond, 1.0, 0.0).astype(BF16)


def dot_nn(a, b):
    return lax.dot_general(a, b, (((1,), (0,)), ((), ())), preferred_element_type=F32)


def dot_nt(a, b):
    return lax.dot_general(a, b, (((1,), (1,)), ((), ())), preferred_element_type=F32)


def seat(pos):
    return jnp.where(pos < 5, pos, 20 - pos) if not isinstance(pos, int) else pos if pos < 5 else 20 - pos


def iota(shape, dim):
    return lax.broadcasted_iota(jnp.int32, shape, dim)


def kernel(
    emb_hbm, lab_hbm, out_ref,
    emb, lab, unit, raw, meta, near_out, far_out, opp_out, blocks, pext, ext_in, own, sib, left, acc, colacc,
    tot, wts,
    in_sem, known, raw_send, raw_recv, near_send, far_send, opp_send, meta_send, meta_recv, own_recv,
    ext_send, ext_recv, sib_send, sib_recv, tot_send, tot_recv,
):
    p = lax.axis_index("shard")
    y = lax.axis_index("split")
    z = p >> 3
    x = (p >> 1) & 3
    c = p & 1
    xy = x * NY + y
    turn = (y - x + NY) & 3
    handles = (turn & 1) == 0
    my_owner = x * 2 + (turn >> 1)

    def at(zz, xx, cc, yy):
        return (zz * 8 + xx * 2 + cc, yy)

    def handler_y(j):
        return (2 * (j & 1) + (j >> 1)) & 3

    def up(pos):
        k = (pos + 1) >> 1
        return (z + jnp.where((pos & 1) == 1, k, NZ - k)) & (NZ - 1)

    def down(pos):
        k = (pos + 1) >> 1
        return (z + jnp.where((pos & 1) == 1, NZ - k, k)) & (NZ - 1)

    barrier = pltpu.get_barrier_semaphore()
    z_by = lambda k: at((z + k + NZ) & (NZ - 1), x, c, y)
    x_by = lambda k: at(z, (x + k) & 3, c, y)
    y_by = lambda k: at(z, x, c, (y + k) & 3)
    near = [z_by(1), z_by(-1), x_by(1), x_by(3), y_by(1), y_by(3)]
    for device in near + [at(z, x, 1 - c, y)]:
        pl.semaphore_signal(barrier, inc=1, device_id=device, device_id_type=MESH)
    load_emb = pltpu.make_async_copy(emb_hbm, emb, in_sem.at[0])
    load_lab = pltpu.make_async_copy(lab_hbm, lab, in_sem.at[1])
    load_lab.start()
    load_emb.start()

    rounds = [
        near,
        [z_by(2), z_by(-2)],
        [z_by(4), z_by(-4)],
        [y_by(1), y_by(2), y_by(3)],
        [x_by(1), x_by(2), x_by(3)],
    ]

    def tell(r):
        for device in rounds[r]:
            pl.semaphore_signal(known.at[r], inc=1, device_id=device, device_id_type=MESH)

    def learn(r):
        pl.semaphore_wait(known.at[r], len(rounds[r]))

    load_lab.wait()
    load_emb.wait()
    wide = emb[...].astype(F32)
    norm_sq = jnp.sum(wide * wide, axis=1, keepdims=True) + 1e-06
    unit[...] = (wide * lax.rsqrt(norm_sq)).astype(BF16)
    label = lab[...]
    owner = label >> 3
    owner_f = jnp.broadcast_to(owner.astype(F32), (ROWS, ROWS))
    earlier = (owner_f == owner_f.T) & (iota((ROWS, ROWS), 0) < iota((ROWS, ROWS), 1))
    rank = jnp.sum(jnp.where(earlier, 1.0, 0.0), axis=0, keepdims=True).astype(jnp.int32)
    meta[0] = label * 4 + rank

    pl.semaphore_wait(barrier, 7)

    def raw_copy(way, hop, piece):
        rows = pl.ds(piece * PIECE, PIECE)
        src = unit.at[rows] if hop == 0 else raw.at[way, 0, rows]
        to = (z + (1 if way == 0 else NZ - 1)) & (NZ - 1)
        return pltpu.make_async_remote_copy(
            src_ref=src, dst_ref=raw.at[way, hop, rows],
            send_sem=raw_send.at[way, hop, piece], recv_sem=raw_recv.at[way, hop, piece],
            device_id=at(to, x, c, y), device_id_type=MESH,
        )

    pieces = ROWS // PIECE
    for piece in range(pieces):
        for way in range(2):
            raw_copy(way, 0, piece).start()

    def meta_copy(pos, sem):
        return pltpu.make_async_remote_copy(
            src_ref=meta.at[0], dst_ref=meta.at[pos],
            send_sem=meta_send.at[pos], recv_sem=meta_recv.at[sem],
            device_id=at(up(pos), x, c, y), device_id_type=MESH,
        )

    meta_copy(1, 0).start()
    meta_copy(2, 0).start()
    tell(0)
    learn(0)
    meta_copy(3, 0).start()
    meta_copy(4, 0).start()
    tell(1)
    learn(1)
    tell(2)

    def slots_of(code):
        return ((code >> 5) << 2) | (code & 3)

    def to_blocks(code, first, count, rows):
        line = iota((8 * count, ROWS), 0)
        pick = one_hot(slots_of(code) == ((first(line >> 3) << 2) | (line & 3)))
        twice = dot_nn(pick, rows)
        upper = (iota((8 * count, 128), 0) & 4) == 0
        thirds = [
            jnp.where(upper, twice[:, k : k + 128], twice[:, k + 128 : k + 256]).reshape(count, 8, 128)
            for k in range(0, D, 256)
        ]
        return jnp.concatenate(thirds, axis=1).astype(BF16)

    def is_here(j):
        return jnp.logical_and((j >> 1) == x, handler_y(j) == y)

    def handler(zz, j):
        return at(zz, (j >> 1), c, handler_y(j))

    def block_copy(src, pos, zz, j, sem):
        return pltpu.make_async_remote_copy(
            src_ref=src, dst_ref=blocks.at[pos, xy], send_sem=sem, recv_sem=own_recv.at[pos],
            device_id=handler(zz, j), device_id_type=MESH,
        )

    def near_copy(pos, j):
        return block_copy(near_out.at[pos, j], pos, z, j, near_send.at[pos, j])

    def far_plane(way, g):
        return (z + (1 + g if way == 0 else NZ - 1 - g)) & (NZ - 1)

    def far_copy(way, g, j):
        return block_copy(far_out.at[way, g * 8 + j], 2 * g + 5 + way, far_plane(way, g), j, far_send.at[way])

    def opp_copy(way, j):
        zz = (z + (7 if way == 0 else NZ - 7)) & (NZ - 1)
        return block_copy(opp_out.at[way, j], 15, zz, way * 4 + j, opp_send.at[way])

    def send_near(pos, rows_ref):
        near_out[pos] = to_blocks(meta[pos], lambda j: z * 8 + j, 8, rows_ref[...])

        def send(j, _):
            @pl.when(is_here(j))
            def _():
                pltpu.make_async_copy(near_out.at[pos, j], blocks.at[pos, xy], own_recv.at[pos]).start()

            @pl.when(jnp.logical_not(is_here(j)))
            def _():
                near_copy(pos, j).start()
            return 0

        lax.fori_loop(0, 8, send, 0)

    for piece in range(pieces):
        for way in range(2):
            raw_copy(way, 0, piece).wait_recv()
            raw_copy(way, 1, piece).start()
        if piece == 0:
            learn(2)
            tell(3)
    near_meta = meta.at[pl.ds(1, 4)]
    pltpu.make_async_copy(near_meta, near_meta, meta_recv.at[0]).wait()
    learn(3)
    tell(4)

    def meta_start(pos, _):
        meta_copy(pos, 1).start()
        return 0

    lax.fori_loop(5, NZ, meta_start, 0)
    for way in range(2):
        zz = (z + (7 if way == 0 else NZ - 7)) & (NZ - 1)
        first = functools.partial(lambda base, j: base + j, zz * 8 + way * 4)
        opp_out[way] = to_blocks(meta[1 + way], first, 4, raw[way, 0])
    learn(4)
    for way in range(2):
        for j in range(4):
            opp_copy(way, j).start()
    send_near(0, unit)
    send_near(1, raw.at[0, 0])
    send_near(2, raw.at[1, 0])

    for way in range(2):
        for piece in range(pieces):
            raw_copy(way, 1, piece).wait_recv()

        def first(i, way=way):
            step = 1 + (i >> 3)
            return (((z + (step if way == 0 else NZ - step)) & (NZ - 1)) << 3) + (i & 7)

        far_out[way] = to_blocks(meta[3 + way], first, 40, raw[way, 1])

        for g in (4, 3, 2, 1, 0):
            def far_start(j, _, g=g, way=way):
                far_copy(way, g, j).start()
                return 0

            lax.fori_loop(0, 8, far_start, 0, unroll=True)

    send_near(3, raw.at[0, 1])
    send_near(4, raw.at[1, 1])

    i128 = iota((ROWS, ROWS), 0)
    lane = iota((ROWS, ROWS), 1)
    zq, j4 = (i128 >> 2) & 3, ((i128 >> 4) << 2) | (i128 & 3)

    def mine16():
        return pl.ds(pl.multiple_of(xy * 16, 16), 16)

    def ext_copy(j):
        return pltpu.make_async_remote_copy(
            src_ref=pext.at[j], dst_ref=ext_in.at[:, mine16()],
            send_sem=ext_send.at[j], recv_sem=ext_recv,
            device_id=at(z, (j >> 1), c, handler_y(j)), device_id_type=MESH,
        )

    far_meta = meta.at[pl.ds(5, NZ - 5)]
    pltpu.make_async_copy(far_meta, far_meta, meta_recv.at[1]).wait()
    for q in range(4):
        same = jnp.zeros((ROWS, EXT), F32)
        for k in range(4):
            code = meta[seat(q * 4 + k)]
            pick = one_hot((slots_of(code) == z * 32 + j4) & (zq == k))
            same += dot_nt(pick, one_hot((((code >> 2) & 7) == i128) | (i128 == 8)))
        right = jnp.where(lane < 8, PENALTY * same - PENALTY, jnp.where(lane == 8, -PENALTY * same, 0.0))
        pext[:, q] = right.astype(BF16).reshape(8, 16, EXT)

    def ext_start(j, _):
        @pl.when(is_here(j))
        def _():
            pltpu.make_async_copy(pext.at[j], ext_in.at[:, mine16()], ext_recv).start()

        @pl.when(jnp.logical_not(is_here(j)))
        def _():
            ext_copy(j).start()
        return 0

    lax.fori_loop(0, 8, ext_start, 0)

    def sib_copy(q, g):
        rows = pl.ds(pl.multiple_of(g * 64, 64), 64)
        return pltpu.make_async_remote_copy(
            src_ref=own.at[q, rows], dst_ref=sib.at[q, rows],
            send_sem=sib_send.at[q, g], recv_sem=sib_recv.at[q, g],
            device_id=at(z, x, 1 - c, y), device_id_type=MESH,
        )

    def terms(left_rows, right_rows):
        return jnp.exp2(dot_nt(left_rows, right_rows) * LOG2E10)

    def lane_sums(e):
        total = e[:, :128]
        for k in range(1, e.shape[1] // 128):
            total = total + e[:, k * 128 : k * 128 + 128]
        return total

    def permute_lanes():
        pltpu.make_async_copy(ext_in, ext_in, ext_recv).wait()
        row, col = iota((256, 256), 0), iota((256, 256), 1)
        order = one_hot(col == (((row >> 2) & 15) << 4) + ((row >> 6) << 2) + (row & 3))
        for k in range(4):
            own[k, :, D:] = dot_nn(order, ext_in[k]).astype(BF16)

    def take(q):
        row, col = iota((384, 384), 0), iota((384, 384), 1)
        line = ((row >> 2) & 15) * 24 + ((row >> 6) << 2) + (row & 3)
        unpack = one_hot(col == line)

        def one(k, _):
            pos = seat(q * 4 + k)
            pltpu.make_async_copy(blocks.at[pos], blocks.at[pos], own_recv.at[pos]).wait()
            lines = blocks[pos].astype(F32).reshape(384, 128).astype(BF16)
            parts = dot_nn(unpack, lines).astype(BF16)
            here = pl.ds(pl.multiple_of(k * 64, 64), 64)
            for i in range(6):
                own[q, here, i * 128 : i * 128 + 128] = parts[i * 64 : i * 64 + 64]
            sib_copy(q, k).start()
            return 0

        lax.fori_loop(0, 4, one, 0)

    def own_sums(q):
        old, new = q * 256, q * 256 + 256
        left[old:new, :D] = own[q, :, :D]
        is_cluster = iota((256, EXT), 1) < 9
        left[old:new, D:] = jnp.where(
            is_cluster, own[q, :, D:].astype(F32) * (1.0 / PENALTY) + 1.0, 0.0
        ).astype(BF16)
        e = terms(left[:new, :], own[q])
        sums = lane_sums(e)
        acc[old:new, :] = sums[old:]
        if q:
            acc[:old, :] = acc[:old, :] + sums[:old]
            colacc[q] = jnp.sum(e[:old].reshape(old // 8, 8, 256), axis=0)
        else:
            colacc[q] = jnp.zeros((8, 256), F32)

    def sib_sums(q):
        old, new = q * 256, q * 256 + 256

        def sib_wait(g, _):
            sib_copy(q, g).wait_recv()
            return 0

        lax.fori_loop(0, 4, sib_wait, 0)
        acc[:new, :] = acc[:new, :] + lane_sums(terms(left[:new, :], sib[q]))
        if q:
            e = terms(left[old:new, :], sib[:q].reshape(old, WIDE))
            acc[old:new, :] = acc[old:new, :] + lane_sums(e)

    @pl.when(handles)
    def _():
        permute_lanes()
        take(0)
        take(1)
        own_sums(0)
        own_sums(1)
        sib_sums(0)
        take(2)
        own_sums(2)
        sib_sums(1)
        take(3)
        sib_sums(2)
        own_sums(3)
        sib_sums(3)

    def tot_copy(i):
        pos, to = 15 - (i >> 4), i & 15
        return pltpu.make_async_remote_copy(
            src_ref=tot.at[seat(pos) >> 1], dst_ref=wts.at[z * 8 + my_owner],
            send_sem=tot_send, recv_sem=tot_recv,
            device_id=at(down(pos), to >> 2, c, to & 3), device_id_type=MESH,
        )

    @pl.when(handles)
    def _():
        for q in range(4):
            for h in range(2):
                part = acc[pl.ds(q * 256 + h * 128, 128), :].T
                total = jnp.sum(part, axis=0, keepdims=True) + jnp.sum(
                    colacc[q, :, h * 128 : h * 128 + 128], axis=0, keepdims=True
                )
                tot[q * 2 + h] = total

        def send(i, _):
            tot_copy(i).start()
            return 0

        def send_here(i, _):
            @pl.when(i - 240 != xy)
            def _():
                tot_copy(i).start()
            return 0

        lax.fori_loop(0, 240, send, 0, unroll=8)
        pltpu.make_async_copy(tot.at[0], wts.at[z * 8 + my_owner], tot_recv).start()
        lax.fori_loop(240, 256, send_here, 0)

    arrived = wts.at[pl.ds(0, NZ * 8)]
    pltpu.make_async_copy(arrived, arrived, tot_recv).wait()

    code = meta[0]
    table = wts[: NZ * 8].reshape(NZ * 8, 128).T
    lines = jnp.where((code >> 5) == iota((NZ * 8, ROWS), 0), 1.0, 0.0)
    picked = jnp.dot(table, lines, precision=lax.Precision.HIGHEST, preferred_element_type=F32)
    ahead = ((code >> 8) - z) & (NZ - 1)
    pos = jnp.where(ahead == 0, 0, jnp.where(ahead <= 8, 2 * ahead - 1, 2 * (NZ - ahead)))
    lane = (seat(pos) & 1) * 64 + xy * 4 + (code & 3)
    total = jnp.sum(jnp.where(iota((128, ROWS), 0) == lane, picked, 0.0), axis=0, keepdims=True)
    out_ref[...] = 0.1 * jnp.log(total)

    for way in range(2):
        for hop in range(2):
            for piece in range(pieces):
                raw_copy(way, hop, piece).wait_send()
        pltpu.make_async_copy(far_out.at[way], far_out.at[way], far_send.at[way]).wait()
        pltpu.make_async_copy(opp_out.at[way], opp_out.at[way], opp_send.at[way]).wait()

    def drain_z(pos, _):
        meta_copy(pos, 0).wait_send()
        return 0

    lax.fori_loop(1, NZ, drain_z, 0)

    def drain_plane(j, _):
        @pl.when(jnp.logical_not(is_here(j)))
        def _():
            ext_copy(j).wait_send()
            for pos in range(5):
                near_copy(pos, j).wait_send()
        return 0

    lax.fori_loop(0, 8, drain_plane, 0)

    @pl.when(handles)
    def _():
        def drain_sib(k, _):
            sib_copy(k >> 2, k & 3).wait_send()
            return 0

        lax.fori_loop(0, 16, drain_sib, 0)

        sent = wts.at[pl.ds(0, 255)]
        pltpu.make_async_copy(sent, sent, tot_send).wait()


def per_device(embeddings, labels):
    dma = pltpu.SemaphoreType.DMA
    vmem = pltpu.VMEM
    weight = pl.pallas_call(
        kernel,
        out_shape=jax.ShapeDtypeStruct((1, ROWS), F32),
        in_specs=[pl.BlockSpec(memory_space=pltpu.HBM)] * 2,
        out_specs=pl.BlockSpec(memory_space=pltpu.VMEM),
        scratch_shapes=[
            vmem((ROWS, D), BF16),
            vmem((1, ROWS), jnp.int32),
            vmem((ROWS, D), BF16),
            vmem((2, 2, ROWS, D), BF16),
            vmem((NZ, 1, ROWS), jnp.int32),
            vmem((5, 8, 24, 128), BF16),
            vmem((2, 40, 24, 128), BF16),
            vmem((2, 4, 24, 128), BF16),
            vmem((NZ, 16, 24, 128), BF16),
            vmem((8, 4, 16, EXT), BF16),
            vmem((4, 256, EXT), BF16),
            vmem((4, 256, WIDE), BF16),
            vmem((4, 256, WIDE), BF16),
            vmem((1024, WIDE), BF16),
            vmem((1024, 128), F32),
            vmem((4, 8, 256), F32),
            vmem((8, 1, 128), F32),
            vmem((2 * NZ * 8, 1, 128), F32),
            dma((2,)), pltpu.SemaphoreType.REGULAR((5,)),
            dma((2, 2, ROWS // PIECE)), dma((2, 2, ROWS // PIECE)),
            dma((5, 8)), dma((2,)), dma((2,)),
            dma((NZ,)), dma((2,)),
            dma((NZ,)),
            dma((8,)), dma,
            dma((4, 4)), dma((4, 4)),
            dma, dma,
        ],
        compiler_params=pltpu.CompilerParams(
            collective_id=0, has_side_effects=True, vmem_limit_bytes=64 * 1024 * 1024
        ),
        name="soft_dedup",
    )(embeddings, labels.reshape(1, ROWS))
    return weight.reshape(ROWS)


def solution(mesh):
    placed = (P(("shard", "split"), None), P(("shard", "split")))
    return jax.shard_map(
        per_device, mesh=mesh, in_specs=placed, out_specs=P(("shard", "split")), check_vma=False
    )
```
